256 devices in a mesh: phase: 4 (over y), elem: 64 (over x, z, core).
Axes of the slice: x: 4, y: 4, z: 8, core: 2. Of those that a mesh axis runs over, the one named last changes fastest.
Arguments:
- state: bfloat16 [131072, 320], P(('phase', 'elem')), parts along dimension 0, may hold values from -6 to 6
- adjoint: bfloat16 [131072, 320], P(('phase', 'elem')), parts along dimension 0, may hold values from -6 to 6
- right_side: bfloat16 [131072, 320], P(('phase', 'elem')), parts along dimension 0, may hold values from -6 to 6
- source: bfloat16 [131072, 320], P(('phase', 'elem')), parts along dimension 0, may hold values from -6 to 6
- metric: float32 [8, 32768], P(None, 'elem'), may hold values from 0.5 to 2
- basis_tiles: bfloat16 [32, 320, 320], P('phase'), parts along dimension 0, may hold values from -0.125 to 0.125
- face_tiles: bfloat16 [24, 320, 320], P('phase'), parts along dimension 0, may hold values from -0.125 to 0.125
- precond: bfloat16 [1280, 320], P('phase'), parts along dimension 0, may hold values from -0.3125 to 0.3125
- wall_tile: bfloat16 [512, 320], P('phase'), parts along dimension 0, may hold values from -0.5 to 0.5
- traction_tile: bfloat16 [1280, 128], P('phase'), parts along dimension 0, may hold values from -0.3125 to 0.3125
- mode_rows: bfloat16 [65536, 128], P(('phase', 'elem')), parts along dimension 0, may hold values from -6 to 6
- neighbors: int32 [32768, 6], P('elem'), may hold values from -1 to 32767, as said below
- wall_node: int32 [32768], P('elem'), may hold values from -1 to 16383, as said below
- wall_target: int32 [16384], P('elem'), may hold values from 0 to 32767, as said below
Outputs:
- new_state: bfloat16 [131072, 320], P(('phase', 'elem')), parts along dimension 0
- new_adjoint: bfloat16 [131072, 320], P(('phase', 'elem')), parts along dimension 0
- wall_load: bfloat16 [65536, 128], P(('phase', 'elem')), parts along dimension 0
The draws below stay inside these ranges and needn't reach their ends.
There are 4 independent parts, one for each index of `phase`. The reference program is written for one: setup_inputs(seed, part) draws one part's arguments, and reference() takes and returns one part's arrays. A program takes and returns all parts, laid end to end along the dimension named above; an argument that names none is the same for every part. Nothing has to cross between parts.
Inputs may be any that keep to these rules, and one draw needn't show every extreme that they name: `neighbors`: entry (e, f) is -1 where the face lies on the slab boundary, else an element at most 64 positions from e in the numbering; faces 4 and 5 lie exactly 64 positions away where they exist. `wall_target`: distinct nodes name distinct elements. Of the 256 nodes of one device at most 8 name elements of any one device, and some pair of devices reaches 8. wall_node is the inverse of wall_target: wall_node[wall_target[n]] = n, and -1 on every element that no node names.
All inputs are finite; a program needn't handle non-finite values.
Results may differ from the reference program's by a relative error of at most 0.006.
Values may be sent and summed in bfloat16 or wider, within the bound.
No kernel may reach another device: no remote copies, remote signals or barrier semaphores. Data moves between devices by JAX's collectives and lax.ppermute only.
A program may use at most 64 MiB of HBM per device.

```python
import math
import jax
import jax.numpy as jnp

NVAR = 320
MODE_W = 128
NGEO = 8
NFACE = 6
HALO = 64
ELEM_DEV = 512
WALL_DEV = 256
CAP = 8
NEL = 32768
NODES = 16384


def wall_targets(key):
    count = NEL // ELEM_DEV
    base = jax.random.fold_in(key, 7)
    key_order, key_noise, key_perm = jax.random.split(base, 3)
    heavy_count = max(1, count // 2)
    order = jax.random.permutation(key_order, count)
    heavy = (order < heavy_count).astype(jnp.int32)
    leading = (order == 0).astype(jnp.int32)
    noise = jax.random.randint(key_noise, (count, count, CAP), 0, 1 << 16)
    score = noise + (heavy * (1 << 17) + leading * (1 << 18))[None, :, None]
    width = count * CAP
    flat = score.reshape(count, width) * width + jnp.arange(width, dtype=jnp.int32)[None, :]
    ranked = jnp.argsort(jnp.argsort(-flat, axis=1), axis=1)
    chosen = (ranked < WALL_DEV).astype(jnp.int32).reshape(count, count, CAP)
    taken = jnp.sum(chosen, axis=2)
    ends = jnp.cumsum(taken, axis=1)
    starts = ends - taken
    node_index = jnp.arange(WALL_DEV, dtype=jnp.int32)
    target_dev = jnp.sum((ends[:, None, :] <= node_index[None, :, None]).astype(jnp.int32), axis=2)
    rank = node_index[None, :] - jnp.take_along_axis(starts, target_dev, axis=1)
    perms = jax.vmap(lambda single: jax.random.permutation(single, ELEM_DEV))(jax.random.split(key_perm, count))
    slot = jnp.arange(count, dtype=jnp.int32)[:, None] * CAP + rank
    local = perms[target_dev, slot]
    return (target_dev * ELEM_DEV + local).reshape(NODES).astype(jnp.int32)


def draw_wall_target(key, part):
    return wall_targets(key)


def draw_wall_node(key, part):
    target = wall_targets(key)
    empty = jnp.full((NEL,), -1, jnp.int32)
    return empty.at[target].set(jnp.arange(NODES, dtype=jnp.int32))


def draw_neighbors(key, part):
    inner = jax.random.fold_in(key, 11)
    index = jnp.arange(NEL, dtype=jnp.int32)[:, None]
    jitter = jax.random.randint(inner, (NEL, 4), 1, HALO)
    signs = jnp.array([1, -1, 1, -1], jnp.int32)
    planes = jnp.full((NEL, 2), HALO, jnp.int32) * jnp.array([1, -1], jnp.int32)[None, :]
    reach = jnp.concatenate([jitter * signs[None, :], planes], axis=1)
    other = index + reach
    return jnp.where((other >= 0) & (other < NEL), other, -1).astype(jnp.int32)


def block_scale(own_key, dims, pieces, least, high):
    level = 1.0
    for dim, parts in pieces:
        draws = jax.random.uniform(jax.random.fold_in(jax.random.fold_in(own_key, 6), dim), (parts,), jnp.float32, least / len(pieces), high / len(pieces))
        level = level * jnp.repeat(jnp.exp(draws), dims[dim] // parts).reshape((-1,) + (1,) * (len(dims) - 1 - dim))
    return level


def normal_values(key, extent, scale, bound, pieces=(), kind=jnp.bfloat16):
    factor_of = block_scale(key, extent, pieces, -0.22, 0.18) if pieces else 1.0
    values = jax.random.normal(key, extent, jnp.float32) * scale * factor_of
    return jnp.minimum(jnp.maximum(values, -bound), bound).astype(kind)


def setup_inputs(seed: int = 0, part: int = 0) -> dict:
    seeds = jax.random.split(jax.random.key(seed), 15)
    part_splits = jax.random.split(jax.random.fold_in(seeds[14], part), 15)
    return {
        "state": normal_values(part_splits[0], (NEL, NVAR), 1.0, 6.0, ((0, 64),)),
        "adjoint": normal_values(part_splits[1], (NEL, NVAR), 1.0, 6.0, ((0, 64),)),
        "right_side": normal_values(part_splits[2], (NEL, NVAR), 1.0, 6.0, ((0, 64),)),
        "source": normal_values(part_splits[3], (NEL, NVAR), 1.0, 6.0, ((0, 64),)),
        "metric": jnp.clip(jnp.exp(math.log(2.0) - 1.3862944 * jax.random.uniform(seeds[4], (NGEO, NEL), jnp.float32) ** block_scale(seeds[4], (NGEO, NEL), ((1, 64),), -0.2, 0.2)), 0.5, 2.0),
        "basis_tiles": normal_values(part_splits[5], (NGEO, NVAR, NVAR), (NVAR * NGEO) ** -0.5, 0.125),
        "face_tiles": normal_values(part_splits[6], (NFACE, NVAR, NVAR), (NVAR * NFACE) ** -0.5, 0.125),
        "precond": normal_values(part_splits[7], (NVAR, NVAR), NVAR ** -0.5, 0.3125),
        "wall_tile": normal_values(part_splits[8], (MODE_W, NVAR), MODE_W ** -0.5, 0.5),
        "traction_tile": normal_values(part_splits[9], (NVAR, MODE_W), NVAR ** -0.5, 0.3125),
        "mode_rows": normal_values(part_splits[10], (NODES, MODE_W), 1.0, 6.0, ((0, 64),)),
        "neighbors": draw_neighbors(jax.random.fold_in(seeds[14], 71), part),
        "wall_node": draw_wall_node(jax.random.fold_in(seeds[14], 71), part),
        "wall_target": draw_wall_target(jax.random.fold_in(seeds[14], 71), part),
    }


def reference(state, adjoint, right_side, source, metric, basis_tiles, face_tiles, precond, wall_tile, traction_tile, mode_rows, neighbors, wall_node, wall_target):
    on_wall = wall_node >= 0
    picked = mode_rows[jnp.maximum(wall_node, 0).astype(jnp.int32)]
    wall_modes = jnp.where(on_wall[:, None], picked, jnp.zeros((), jnp.bfloat16))
    factors = jnp.transpose(metric)
    basis_wide = basis_tiles.astype(jnp.float32)
    faces_wide = face_tiles.astype(jnp.float32)
    linked = neighbors >= 0
    safe_index = jnp.clip(neighbors, 0, NEL - 1).astype(jnp.int32)

    diagonal = jnp.einsum("ew,kwv->ekv", state.astype(jnp.float32), basis_wide)
    applied = jnp.sum(diagonal * factors[:, :, None], axis=1)
    beside = jnp.where(linked[:, :, None], state[safe_index], jnp.zeros((), jnp.bfloat16))
    applied = applied + jnp.einsum("efw,fwv->ev", beside.astype(jnp.float32), faces_wide)
    forcing = jnp.dot(wall_modes, wall_tile, preferred_element_type=jnp.float32)
    residual = (right_side.astype(jnp.float32) + forcing - applied).astype(jnp.bfloat16)
    update = jnp.dot(residual, precond, preferred_element_type=jnp.float32)
    new_state = (state.astype(jnp.float32) + update / factors[:, 0:1]).astype(jnp.bfloat16)

    diagonal_t = jnp.einsum("ew,kvw->ekv", adjoint.astype(jnp.float32), basis_wide)
    applied_t = jnp.sum(diagonal_t * factors[:, :, None], axis=1)
    pushed = jnp.einsum("ew,fvw->efv", adjoint.astype(jnp.float32), faces_wide)
    pushed = pushed * linked[:, :, None].astype(jnp.float32)
    applied_t = applied_t.at[safe_index].add(pushed)
    adjoint_residual = (source.astype(jnp.float32) - applied_t).astype(jnp.bfloat16)
    update_t = jnp.dot(adjoint_residual, jnp.transpose(precond), preferred_element_type=jnp.float32)
    new_adjoint = (adjoint.astype(jnp.float32) + update_t / factors[:, 0:1]).astype(jnp.bfloat16)

    traction = jnp.dot(new_adjoint, traction_tile, preferred_element_type=jnp.float32).astype(jnp.bfloat16)
    wall_load = traction[wall_target.astype(jnp.int32)]
    return (new_state, new_adjoint, wall_load)
```

```python
import jax
import jax.numpy as jnp
from jax import lax
from jax.experimental import pallas as pl
from jax.experimental.pallas import tpu as pltpu
from jax.sharding import PartitionSpec as P

HALO = 64
BLOCK = 128
MAIN = 256
CAP = 8
F32 = jnp.float32
BF16 = jnp.bfloat16
NT = (((1,), (1,)), ((), ()))


def columns_of(rows, count):
    padded = jnp.concatenate([rows] + [jnp.zeros_like(rows)] * (128 // rows.shape[0] - 1), axis=0)
    return jnp.transpose(padded)


def diagonal_kernel(
    state_ref,
    adjoint_ref,
    metric_ref,
    basis_ref,
    wall_node_ref,
    wall_target_ref,
    diag_ref,
    diag_t_ref,
    srow_ref,
    scol_ref,
    x_ref,
    w_ref,
):
    elems, width = state_ref.shape
    count = basis_ref.shape[0]
    tail = width - MAIN
    factors = columns_of(metric_ref[...], elems)

    def scaled_into(value_ref):
        value = value_ref[...].astype(F32)
        main, rest = value[:, :MAIN], value[:, MAIN:]
        tails = []
        for k in range(count):
            x_ref[:, k * MAIN : (k + 1) * MAIN] = (main * factors[:, k : k + 1]).astype(BF16)
            tails.append((rest * factors[:, k : k + 1]).astype(BF16))
        x_ref[:, count * MAIN :] = jnp.concatenate(tails, axis=1)

    scaled_into(state_ref)
    for k in range(count):
        w_ref[k * MAIN : (k + 1) * MAIN, :] = basis_ref[k, :MAIN, :]
        w_ref[count * MAIN + k * tail : count * MAIN + (k + 1) * tail, :] = basis_ref[k, MAIN:, :]
    diag_ref[...] = jnp.dot(x_ref[...], w_ref[...], preferred_element_type=F32)

    scaled_into(adjoint_ref)
    total = lax.dot_general(
        x_ref[:, count * MAIN :],
        jnp.concatenate([basis_ref[k, :, MAIN:] for k in range(count)], axis=1),
        NT,
        preferred_element_type=F32,
    )
    for k in range(count):
        total += lax.dot_general(
            x_ref[:, k * MAIN : (k + 1) * MAIN],
            basis_ref[k, :, :MAIN],
            NT,
            preferred_element_type=F32,
        )
    diag_t_ref[...] = total

    def slots(device_row, order_row):
        n = device_row.shape[1]
        device_col = jnp.transpose(jnp.broadcast_to(device_row, (128, n)))[:, :1]
        order_col = jnp.transpose(jnp.broadcast_to(order_row, (128, n)))[:, :1]
        same = device_col == device_row
        before = jnp.where(same & (order_col < order_row), 1.0, 0.0)
        after = jnp.where(same & (order_row < order_col), 1.0, 0.0)
        row = device_row * CAP + jnp.sum(before, axis=0, keepdims=True)
        col = device_col * CAP + jnp.sum(after, axis=1, keepdims=True)
        return row, col

    nodes = wall_target_ref.shape[1]
    target = wall_target_ref[...]
    node_order = lax.broadcasted_iota(jnp.int32, (1, nodes), 1).astype(F32)
    node_row, node_col = slots((target // elems).astype(F32), node_order)
    node = wall_node_ref[...]
    owner = jnp.where(node >= 0, node // nodes, -1).astype(F32)
    elem_row, elem_col = slots(owner, node.astype(F32))
    srow_ref[...] = jnp.zeros(srow_ref.shape, F32)
    srow_ref[0:1, :] = elem_row
    srow_ref[1:2, :nodes] = node_row
    scol_ref[0] = elem_col
    scol_ref[1, :nodes] = node_col


def faces_kernel(
    state_ref,
    adjoint_ref,
    right_ref,
    source_ref,
    metric_ref,
    faces_ref,
    precond_ref,
    traction_tile_ref,
    mode_ref,
    neighbors_ref,
    code_ref,
    before_ref,
    after_ref,
    diag_ref,
    diag_t_ref,
    srow_ref,
    rest_ref,
    new_adjoint_ref,
    send_ref,
    x_ref,
    w_ref,
):
    elems, width = state_ref.shape
    count = faces_ref.shape[0]
    tail = width - MAIN
    offset = width + tail
    blocks = elems // BLOCK

    def window(value_ref, start, b):
        low, high = b * BLOCK - HALO, b * BLOCK + BLOCK + HALO
        parts = []
        if low < 0:
            parts.append(before_ref[:, start : start + width])
        parts.append(value_ref[max(low, 0) : min(high, elems), :])
        if high > elems:
            parts.append(after_ref[:, start : start + width])
        return parts[0] if len(parts) == 1 else jnp.concatenate(parts, axis=0)

    def place(b, gathered):
        rows = slice(b * BLOCK, (b + 1) * BLOCK)
        tails = []
        for f in range(count):
            one = gathered[f * BLOCK : (f + 1) * BLOCK, :]
            x_ref[rows, f * MAIN : (f + 1) * MAIN] = one[:, :MAIN]
            tails.append(one[:, MAIN:])
        x_ref[rows, count * MAIN :] = jnp.concatenate(tails, axis=1)

    own = code_ref[...].astype(F32)
    pad = jnp.zeros((elems, 128 - own.shape[1]), F32)
    own_rows = jnp.transpose(jnp.concatenate([own, pad], axis=1))[:8, :]
    zero_side = jnp.zeros((HALO, 2 * HALO), F32)
    low_rows = jnp.transpose(
        jnp.concatenate([before_ref[:, width : width + tail].astype(F32), zero_side[:, :HALO]], axis=1)
    )[:8, :]
    high_rows = jnp.transpose(
        jnp.concatenate([after_ref[:, width : width + tail].astype(F32), zero_side[:, :HALO]], axis=1)
    )[:8, :]
    codes = jnp.concatenate([low_rows, own_rows, high_rows], axis=1)
    codes = jnp.where(codes == 0.0, -1000.0, codes)
    span = BLOCK + 2 * HALO
    lane = lax.broadcasted_iota(jnp.int32, (8, span), 1).astype(F32)
    place_row = lax.broadcasted_iota(jnp.int32, (BLOCK, span), 0).astype(F32)
    place_lane = lax.broadcasted_iota(jnp.int32, (BLOCK, span), 1)
    for b in range(blocks):
        targets = codes[:, b * BLOCK : b * BLOCK + span] + lane - (2.0 * HALO + 1.0)
        hot = jnp.concatenate(
            [
                jnp.where(place_row == targets[f : f + 1, :], 1.0, 0.0).astype(BF16)
                for f in range(count)
            ],
            axis=0,
        )
        place(
            b,
            jnp.dot(hot, window(adjoint_ref, offset, b), preferred_element_type=F32).astype(BF16),
        )
    total = lax.dot_general(
        x_ref[:, count * MAIN :],
        jnp.concatenate([faces_ref[f, :, MAIN:] for f in range(count)], axis=1),
        NT,
        preferred_element_type=F32,
    )
    for f in range(count):
        total += lax.dot_general(
            x_ref[:, f * MAIN : (f + 1) * MAIN],
            faces_ref[f, :, :MAIN],
            NT,
            preferred_element_type=F32,
        )
    factor = columns_of(metric_ref[...], elems)[:, :1]
    residual_t = (source_ref[...].astype(F32) - (diag_t_ref[...] + total)).astype(BF16)
    update_t = lax.dot_general(residual_t, precond_ref[...], NT, preferred_element_type=F32)
    new_adjoint = (adjoint_ref[...].astype(F32) + update_t / factor).astype(BF16)
    new_adjoint_ref[...] = new_adjoint
    traction = jnp.dot(new_adjoint, traction_tile_ref[...], preferred_element_type=F32).astype(BF16)

    slots = elems
    elem_hot = jnp.where(
        lax.broadcasted_iota(jnp.int32, (slots, elems), 0).astype(F32) == srow_ref[0:1, :], 1.0, 0.0
    ).astype(BF16)
    nodes = mode_ref.shape[0]
    node_hot = jnp.where(
        lax.broadcasted_iota(jnp.int32, (slots, nodes), 0).astype(F32) == srow_ref[1:2, :nodes],
        1.0,
        0.0,
    ).astype(BF16)
    out_modes = jnp.dot(node_hot, mode_ref[...], preferred_element_type=F32)
    out_traction = jnp.dot(elem_hot, traction, preferred_element_type=F32)
    lanes = out_modes.shape[1]
    send_ref[...] = (
        jnp.concatenate(
            [
                out_modes.reshape(slots // CAP, CAP, lanes),
                out_traction.reshape(slots // CAP, CAP, lanes),
            ],
            axis=1,
        )
        .reshape(2 * slots, lanes)
        .astype(BF16)
    )

    for b in range(blocks):
        local = neighbors_ref[b * BLOCK : (b + 1) * BLOCK, :]
        hot = jnp.concatenate(
            [
                jnp.where(place_lane == local[:, f : f + 1] - b * BLOCK, 1.0, 0.0).astype(BF16)
                for f in range(count)
            ],
            axis=0,
        )
        place(b, jnp.dot(hot, window(state_ref, 0, b), preferred_element_type=F32).astype(BF16))
    for f in range(count):
        w_ref[f * MAIN : (f + 1) * MAIN, :] = faces_ref[f, :MAIN, :]
        w_ref[count * MAIN + f * tail : count * MAIN + (f + 1) * tail, :] = faces_ref[f, MAIN:, :]
    coupled = jnp.dot(x_ref[...], w_ref[...], preferred_element_type=F32)
    rest_ref[...] = right_ref[...].astype(F32) - (diag_ref[...] + coupled)


def finish_kernel(
    state_ref,
    metric_ref,
    precond_ref,
    wall_tile_ref,
    rest_ref,
    scol_ref,
    received_ref,
    new_state_ref,
    wall_load_ref,
):
    elems = state_ref.shape[0]
    nodes = wall_load_ref.shape[0]
    slots = elems
    lanes = received_ref.shape[1]
    received = received_ref[...].astype(F32).reshape(slots // CAP, 2 * CAP, lanes)
    modes = received[:, :CAP, :].reshape(slots, lanes).astype(BF16)
    traction = received[:, CAP:, :].reshape(slots, lanes).astype(BF16)
    elem_hot = jnp.where(
        lax.broadcasted_iota(jnp.int32, (elems, slots), 1).astype(F32) == scol_ref[0], 1.0, 0.0
    ).astype(BF16)
    node_hot = jnp.where(
        lax.broadcasted_iota(jnp.int32, (nodes, slots), 1).astype(F32) == scol_ref[1, :nodes],
        1.0,
        0.0,
    ).astype(BF16)
    wall_load_ref[...] = jnp.dot(node_hot, traction, preferred_element_type=F32).astype(BF16)
    wall_modes = jnp.dot(elem_hot, modes, preferred_element_type=F32).astype(BF16)
    forcing = jnp.dot(wall_modes, wall_tile_ref[...], preferred_element_type=F32)
    residual = (rest_ref[...] + forcing).astype(BF16)
    update = jnp.dot(residual, precond_ref[...], preferred_element_type=F32)
    factor = columns_of(metric_ref[...], elems)[:, :1]
    new_state_ref[...] = (state_ref[...].astype(F32) + update / factor).astype(BF16)


def call(kernel, outs, scratch, flops, args, name):
    spec = pl.BlockSpec(memory_space=pltpu.VMEM)
    size = sum(a.size * a.dtype.itemsize for a in args)
    return pl.pallas_call(
        kernel,
        out_shape=outs,
        in_specs=[spec] * len(args),
        out_specs=[spec] * len(outs),
        scratch_shapes=scratch,
        compiler_params=pltpu.CompilerParams(vmem_limit_bytes=40 * 1024 * 1024),
        cost_estimate=pl.CostEstimate(flops=flops, bytes_accessed=size, transcendentals=0),
        name=name,
    )(*args)


def on_device(
    state,
    adjoint,
    right_side,
    source,
    metric,
    basis_tiles,
    face_tiles,
    precond,
    wall_tile,
    traction_tile,
    mode_rows,
    neighbors,
    wall_node,
    wall_target,
):
    elems, width = state.shape
    nodes, lanes = mode_rows.shape
    geo, faces = basis_tiles.shape[0], face_tiles.shape[0]
    devices = lax.axis_size("elem")
    tail = width - MAIN
    base = lax.axis_index("elem") * elems
    linked = neighbors >= 0
    element = base + lax.broadcasted_iota(jnp.int32, neighbors.shape, 0)
    code = jnp.where(linked, neighbors - element + (HALO + 1), 0).astype(BF16)
    local = jnp.where(linked, neighbors - base + HALO, -1)

    def packed(rows):
        side = jnp.pad(code[rows], ((0, 0), (0, tail - faces)))
        return jnp.concatenate(
            [state[rows], side, adjoint[rows], jnp.zeros((HALO, tail), BF16)], axis=1
        )

    up = [(i, i + 1) for i in range(devices - 1)]
    down = [(j, i) for i, j in up]
    before = lax.ppermute(packed(slice(elems - HALO, elems)), "elem", up)
    after = lax.ppermute(packed(slice(0, HALO)), "elem", down)

    sds = jax.ShapeDtypeStruct
    wide = sds((elems, width), F32)
    narrow = sds((elems, width), BF16)
    diag, diag_t, srow, scol = call(
        diagonal_kernel,
        [wide, wide, sds((8, elems), F32), sds((2, elems, 1), F32)],
        [pltpu.VMEM((elems, geo * width), BF16), pltpu.VMEM((geo * width, width), BF16)],
        4 * geo * elems * width * width,
        (
            state,
            adjoint,
            metric,
            basis_tiles,
            wall_node.reshape(1, elems),
            wall_target.reshape(1, nodes),
        ),
        "diagonal",
    )
    rest, new_adjoint, send = call(
        faces_kernel,
        [wide, narrow, sds((2 * elems, lanes), BF16)],
        [pltpu.VMEM((elems, faces * width), BF16), pltpu.VMEM((faces * width, width), BF16)],
        4 * (faces + 1) * elems * width * width,
        (
            state,
            adjoint,
            right_side,
            source,
            metric,
            face_tiles,
            precond,
            traction_tile,
            mode_rows,
            local,
            code,
            before,
            after,
            diag,
            diag_t,
            srow,
        ),
        "faces",
    )
    received = lax.all_to_all(send, "elem", 0, 0, tiled=True)
    new_state, wall_load = call(
        finish_kernel,
        [narrow, sds((nodes, lanes), BF16)],
        [],
        4 * elems * width * width,
        (state, metric, precond, wall_tile, rest, scol, received),
        "finish",
    )
    return (new_state, new_adjoint, wall_load)


def solution(mesh):
    rows = P(("phase", "elem"), None)
    return jax.shard_map(
        on_device,
        mesh=mesh,
        in_specs=(
            rows,
            rows,
            rows,
            rows,
            P(None, "elem"),
            P("phase", None, None),
            P("phase", None, None),
            P("phase", None),
            P("phase", None),
            P("phase", None),
            rows,
            P("elem", None),
            P("elem"),
            P("elem"),
        ),
        out_specs=(rows, rows, rows),
        check_vma=False,
    )
```

```python
import jax
import jax.numpy as jnp
from jax import lax
from jax.experimental import pallas as pl
from jax.experimental.pallas import tpu as pltpu
from jax.sharding import PartitionSpec as P

HALO = 64
LANES = 128
MAIN = 256
CAP = 8
NOWHERE = -1000.0
F32 = jnp.float32
BF16 = jnp.bfloat16
NT = (((1,), (1,)), ((), ()))


def mm(left, right):
    return jnp.dot(left, right, preferred_element_type=F32)


def mm_nt(left, right):
    return lax.dot_general(left, right, NT, preferred_element_type=F32)


def lane(rows, width=LANES):
    return lax.broadcasted_iota(jnp.int32, (rows, width), 1)


def hot(left, right):
    return jnp.where(left == right, 1.0, 0.0).astype(BF16)


def half_roll(x):
    return jnp.concatenate([x[:, HALO:], x[:, :HALO]], axis=1)


def columns_of(rows):
    fill = jnp.zeros((LANES - rows.shape[0], rows.shape[1]), F32)
    return jnp.transpose(jnp.concatenate([rows, fill], axis=0))


def transposed(x):
    m, n = x.shape
    x = x.astype(F32)
    if m % LANES:
        x = jnp.concatenate([x, jnp.zeros((LANES - m % LANES, n), F32)], axis=0)
    if n % LANES:
        x = jnp.concatenate([x, jnp.zeros((x.shape[0], LANES - n % LANES), F32)], axis=1)
    return jnp.transpose(x)[:n, :m]


def offsets(neighbors, first, elems):
    position = first + lax.broadcasted_iota(jnp.int32, neighbors.shape, 1)
    distance = ((neighbors - position + HALO) & (elems - 1)) - HALO
    return distance, neighbors >= 0, position


def padded_rows(x, rows):
    return jnp.concatenate([x, jnp.zeros((rows - x.shape[0], x.shape[1]), x.dtype)], axis=0)


def key_column(key_row):
    return jnp.transpose(jnp.broadcast_to(key_row, (LANES, key_row.shape[1])))[:, :1]


def rank_row(key_row, base_row):
    column = key_column(key_row)
    return jnp.sum(jnp.where((column < key_row) & (column >= base_row), 1.0, 0.0), axis=0, keepdims=True)


def rank_column(key_row, base_row):
    key, base = key_column(key_row), key_column(base_row)
    return jnp.sum(jnp.where((key_row < key) & (key_row >= base), 1.0, 0.0), axis=1, keepdims=True)


def node_keys(target, elems):
    nodes = target.shape[1]
    device = (target // elems).astype(F32)
    key = device * nodes + lax.broadcasted_iota(jnp.int32, (1, nodes), 1).astype(F32)
    return device, key, device * nodes


def adjoint_halo(parity, same_chip, next_chip):
    mask = (lane(same_chip.shape[0]) < HALO).astype(jnp.int32) != parity
    return jnp.where(mask, next_chip.astype(F32), same_chip.astype(F32))


def state_halo(parity, same_chip, next_chip):
    mask = (lane(same_chip.shape[0]) < HALO).astype(jnp.int32) != parity
    return jnp.where(mask, same_chip.astype(F32), next_chip.astype(F32))


def begin(copies, sems):
    started = [pltpu.make_async_copy(a, b, sems.at[i]) for i, (a, b) in enumerate(copies)]
    for copy in started:
        copy.start()
    return started


def pack_kernel(
    parity_ref,
    state_hbm,
    adjoint_hbm,
    neighbors_hbm,
    same_chip_ref,
    next_chip_ref,
    adjoint_ref,
    neighbors_ref,
    first_ref,
    last_ref,
    sems,
):
    width, elems = adjoint_ref.shape
    final = elems - LANES
    copies = begin(
        [
            (neighbors_hbm, neighbors_ref),
            (state_hbm.at[:, :LANES], first_ref),
            (state_hbm.at[:, final:], last_ref),
            (adjoint_hbm, adjoint_ref),
        ],
        sems,
    )
    low = lane(width) < HALO
    rows = same_chip_ref.shape[0] - width
    copies[0].wait()

    def codes(first):
        distance, linked, _ = offsets(neighbors_ref[:, first : first + LANES], first, elems)
        code = jnp.where(linked, distance + (HALO + 1), 0).astype(F32)
        return half_roll(padded_rows(code, rows)).astype(BF16)

    up_code, down_code = codes(final), codes(0)
    for copy in copies[1:]:
        copy.wait()

    def adjoint(first):
        return half_roll(adjoint_ref[:, first : first + LANES].astype(F32))

    up = jnp.where(low, adjoint(final), last_ref[...].astype(F32)).astype(BF16)
    down = jnp.where(low, first_ref[...].astype(F32), adjoint(0)).astype(BF16)

    @pl.when(parity_ref[0] == 0)
    def _():
        same_chip_ref[:width, :], same_chip_ref[width:, :] = up, up_code
        next_chip_ref[:width, :], next_chip_ref[width:, :] = down, down_code

    @pl.when(parity_ref[0] != 0)
    def _():
        same_chip_ref[:width, :], same_chip_ref[width:, :] = down, down_code
        next_chip_ref[:width, :], next_chip_ref[width:, :] = up, up_code


def spread(x_ref, first, count, lanes, gathered):
    for f in range(count):
        one = gathered[:, f * LANES : (f + 1) * LANES].astype(BF16)
        rest = one.shape[0] - MAIN
        x_ref[first + f * MAIN : first + (f + 1) * MAIN, lanes] = one[:MAIN, :]
        start = first + count * MAIN + f * rest
        x_ref[start : start + rest, lanes] = one[MAIN:, :]


def side_by_side(w_ref, tiles_ref):
    count, width, _ = tiles_ref.shape
    for k in range(count):
        w_ref[:, k * MAIN : (k + 1) * MAIN] = tiles_ref[k, :, :MAIN]
    w_ref[:, count * MAIN :] = jnp.concatenate(
        [tiles_ref[k, :, MAIN:] for k in range(count)], axis=1
    )


def inner_kernel(
    adjoint_ref,
    neighbors_ref,
    source_hbm,
    metric_hbm,
    basis_hbm,
    faces_hbm,
    precond_hbm,
    traction_tile_hbm,
    mode_hbm,
    wall_node_hbm,
    wall_target_hbm,
    partial_ref,
    inner_ref,
    w_faces_ref,
    traction_t_ref,
    srow_ref,
    out_modes_ref,
    out_traction_ref,
    metric_ref,
    basis_ref,
    faces_ref,
    precond_ref,
    x_ref,
    w_ref,
    source_ref,
    traction_tile_ref,
    mode_ref,
    wall_node_ref,
    wall_target_ref,
    sems,
):
    width, elems = adjoint_ref.shape
    geo, count = basis_ref.shape[0], faces_ref.shape[0]
    tail = width - MAIN
    nodes = mode_ref.shape[0]
    copies = begin(
        [
            (metric_hbm, metric_ref),
            (wall_node_hbm, wall_node_ref),
            (wall_target_hbm, wall_target_ref),
            (faces_hbm, faces_ref),
            (basis_hbm, basis_ref),
            (mode_hbm, mode_ref),
            (source_hbm, source_ref),
            (precond_hbm, precond_ref),
            (traction_tile_hbm, traction_tile_ref),
        ],
        sems,
    )
    metric_copy, node_copy, target_copy, faces_copy, basis_copy, mode_copy = copies[:6]

    distance, linked, position = offsets(neighbors_ref[...], 0, elems)
    target = jnp.where(linked, (position + distance).astype(F32), NOWHERE)
    span = LANES + 2 * HALO
    base = geo * width
    for b in range(elems // LANES):
        start = min(max(b * LANES - HALO, 0), elems - span)
        row = b * LANES + lax.broadcasted_iota(jnp.int32, (LANES, span), 0)
        named = jnp.concatenate(
            [hot(row.astype(F32), target[f : f + 1, start : start + span]) for f in range(count)],
            axis=0,
        )
        gathered = mm_nt(adjoint_ref[:, start : start + span], named)
        spread(x_ref, base, count, slice(b * LANES, (b + 1) * LANES), gathered)

    metric_copy.wait()
    value = adjoint_ref[...].astype(F32)
    for k in range(geo):
        scaled = (value * metric_ref[k : k + 1, :]).astype(BF16)
        x_ref[k * MAIN : (k + 1) * MAIN, :] = scaled[:MAIN, :]
        start = geo * MAIN + k * tail
        x_ref[start : start + tail, :] = scaled[MAIN:, :]

    node_copy.wait()
    target_copy.wait()
    node = wall_node_ref[...]
    on_wall = node >= 0
    owner = jnp.where(on_wall, node // nodes, 0).astype(F32)
    elem_slot = owner * CAP + rank_row(node.astype(F32), owner * nodes)
    elem_slot = jnp.where(on_wall, elem_slot, NOWHERE)
    device, key, key_base = node_keys(wall_target_ref[...], elems)
    node_slot = device * CAP + rank_row(key, key_base)
    srow_ref[...] = jnp.zeros(srow_ref.shape, F32)
    srow_ref[0:1, :] = elem_slot
    srow_ref[1:2, :nodes] = node_slot

    faces_copy.wait()
    side_by_side(w_faces_ref, faces_ref)
    total = mm(w_faces_ref[...], x_ref[base:, :])
    basis_copy.wait()
    side_by_side(w_ref, basis_ref)
    total += mm(w_ref[...], x_ref[:base, :])
    for copy in copies[5:]:
        copy.wait()
    rest = source_ref[...].astype(F32) - total
    last = elems - LANES
    partial_ref[:, :LANES] = rest[:, :LANES]
    partial_ref[:, LANES:] = rest[:, last:]

    update = mm(precond_ref[...], rest[:, LANES:last].astype(BF16))
    inverse = 1.0 / metric_ref[0:1, LANES:last]
    inner = (value[:, LANES:last] + update * inverse).astype(BF16)
    inner_ref[...] = inner
    traction_t = transposed(traction_tile_ref[...]).astype(BF16)
    traction_t_ref[...] = traction_t
    traction = mm(traction_t, inner).astype(BF16)

    slots = out_modes_ref.shape[0]
    place = lax.broadcasted_iota(jnp.int32, (slots, nodes), 0).astype(F32)
    out_modes_ref[...] = mm(hot(place, node_slot), mode_ref[...])
    place = lax.broadcasted_iota(jnp.int32, (slots, last - LANES), 0).astype(F32)
    out_traction_ref[...] = mm_nt(hot(place, elem_slot[:, LANES:last]), traction)


def edge_kernel(
    parity_ref,
    same_chip_ref,
    next_chip_ref,
    adjoint_ref,
    metric_ref,
    partial_ref,
    inner_ref,
    w_faces_ref,
    precond_ref,
    traction_t_ref,
    srow_ref,
    out_modes_ref,
    out_traction_ref,
    new_adjoint_ref,
    send_ref,
    x_ref,
):
    width, elems = adjoint_ref.shape
    count = w_faces_ref.shape[1] // width
    last = elems - LANES
    message = adjoint_halo(parity_ref[0], same_chip_ref[...], next_chip_ref[...])
    halo, code = message[:width, :].astype(BF16), message[width : width + 8, :]
    position = lane(8)
    shift = jnp.where(position < HALO, -(2 * HALO + 1), -1)
    target = jnp.where(code == 0.0, NOWHERE, code + (position + shift).astype(F32))
    row = lax.broadcasted_iota(jnp.int32, (LANES, LANES), 0).astype(F32)
    named = jnp.concatenate([hot(row, target[f : f + 1, :]) for f in range(count)], axis=0)
    spread(x_ref, 0, count, slice(0, LANES), mm_nt(halo, named))
    owed = mm(w_faces_ref[...], x_ref[...])
    low = lane(width) < HALO
    rest = jnp.concatenate(
        [
            partial_ref[:, :LANES] - jnp.where(low, owed, 0.0),
            partial_ref[:, LANES:] - jnp.where(low, 0.0, owed),
        ],
        axis=1,
    )
    update = mm(precond_ref[...], rest.astype(BF16))

    def ends(x):
        return jnp.concatenate([x[:, :LANES], x[:, last:]], axis=1)

    inverse = 1.0 / ends(metric_ref[0:1, :])
    edge = (ends(adjoint_ref[...]).astype(F32) + update * inverse).astype(BF16)
    new_adjoint_ref[:, :LANES] = edge[:, :LANES]
    new_adjoint_ref[:, LANES:last] = inner_ref[...]
    new_adjoint_ref[:, last:] = edge[:, LANES:]
    traction = mm(traction_t_ref[...], edge).astype(BF16)
    slots, lanes = out_modes_ref.shape
    place = lax.broadcasted_iota(jnp.int32, (slots, 2 * LANES), 0).astype(F32)
    out_traction = out_traction_ref[...] + mm_nt(hot(place, ends(srow_ref[0:1, :])), traction)
    both = [x.reshape(slots // CAP, CAP, lanes) for x in (out_modes_ref[...], out_traction)]
    send_ref[...] = jnp.concatenate(both, axis=1).reshape(2 * slots, lanes).astype(BF16)


def forward_kernel(
    parity_ref,
    same_chip_ref,
    next_chip_ref,
    metric_ref,
    precond_ref,
    neighbors_ref,
    srow_ref,
    basis_ref,
    faces_ref,
    state_hbm,
    right_hbm,
    wall_tile_t_hbm,
    wall_target_hbm,
    after_hbm,
    most_ref,
    wall_map_ref,
    elem_hot_ref,
    node_hot_ref,
    x_ref,
    w_ref,
    state_ref,
    right_ref,
    wall_tile_t_ref,
    wall_target_ref,
    sems,
):
    width, elems = state_ref.shape
    copies = begin(
        [
            (state_hbm, state_ref),
            (right_hbm, right_ref),
            (wall_tile_t_hbm, wall_tile_t_ref),
            (wall_target_hbm, wall_target_ref),
        ],
        sems,
    )
    copies[0].wait()
    geo, count = basis_ref.shape[0], faces_ref.shape[0]
    tail = width - MAIN
    base = geo * width
    factors = columns_of(metric_ref[...])
    value = transposed(state_ref[...])
    tails = []
    for k in range(geo):
        scaled = (value * factors[:, k : k + 1]).astype(BF16)
        x_ref[:, k * MAIN : (k + 1) * MAIN] = scaled[:, :MAIN]
        tails.append(scaled[:, MAIN:])
    x_ref[:, geo * MAIN : base] = jnp.concatenate(tails, axis=1)

    distance, linked, position = offsets(neighbors_ref[...], 0, elems)
    source = position + distance
    span = LANES + 2 * HALO
    last = elems - LANES
    block = position // LANES
    shift = jnp.where(
        position < LANES,
        jnp.where(source < 0, span, 0),
        jnp.where(
            position >= last,
            jnp.where(source >= elems, -elems, span - elems),
            HALO - block * LANES,
        ),
    )
    column = columns_of(padded_rows(jnp.where(linked, (source + shift).astype(F32), NOWHERE), 8))
    halo = state_halo(parity_ref[0], same_chip_ref[...], next_chip_ref[...])[:width, :].astype(BF16)
    place = lane(LANES, span).astype(F32)
    for b in range(elems // LANES):
        if b == 0:
            beside = jnp.concatenate([state_ref[:, : span - HALO], halo[:, HALO:]], axis=1)
        elif b == elems // LANES - 1:
            beside = jnp.concatenate([halo[:, :HALO], state_ref[:, elems - span + HALO :]], axis=1)
        else:
            beside = state_ref[:, b * LANES - HALO : b * LANES - HALO + span]
        rows = slice(b * LANES, (b + 1) * LANES)
        named = jnp.concatenate([hot(place, column[rows, f : f + 1]) for f in range(count)], axis=0)
        gathered = mm_nt(named, beside).astype(BF16)
        tails = []
        for f in range(count):
            one = gathered[f * LANES : (f + 1) * LANES, :]
            x_ref[rows, base + f * MAIN : base + (f + 1) * MAIN] = one[:, :MAIN]
            tails.append(one[:, MAIN:])
        x_ref[rows, base + count * MAIN :] = jnp.concatenate(tails, axis=1)

    for copy in copies[1:]:
        copy.wait()
    for first, tiles_ref in ((0, basis_ref), (base, faces_ref)):
        number = tiles_ref.shape[0]
        for k in range(number):
            w_ref[first + k * MAIN : first + (k + 1) * MAIN, :] = tiles_ref[k, :MAIN, :]
            start = first + number * MAIN + k * tail
            w_ref[start : start + tail, :] = tiles_ref[k, MAIN:, :]
    applied = mm(x_ref[...], w_ref[...])
    rest = (right_ref[...].astype(F32) - transposed(applied)).astype(BF16)

    precond_t = transposed(precond_ref[...]).astype(BF16)
    inverse = 1.0 / metric_ref[0:1, :]
    most_ref[...] = state_ref[...].astype(F32) + mm(precond_t, rest) * inverse
    wall_map_ref[...] = mm(precond_t, wall_tile_t_ref[...]).astype(BF16)
    slots = elem_hot_ref.shape[0]
    nodes = node_hot_ref.shape[0]
    place = lax.broadcasted_iota(jnp.int32, (slots, elems), 0).astype(F32)
    elem_hot_ref[...] = hot(place, srow_ref[0:1, :])
    device, key, key_base = node_keys(wall_target_ref[...], elems)
    node_slot = key_column(device) * CAP + rank_column(key, key_base)
    node_hot_ref[...] = hot(lane(nodes, slots).astype(F32), node_slot)


def finish_kernel(
    metric_ref,
    most_ref,
    wall_map_ref,
    elem_hot_ref,
    node_hot_ref,
    received_ref,
    new_state_hbm,
    wall_load_hbm,
    new_state_ref,
    wall_load_ref,
    sems,
):
    slots, lanes = elem_hot_ref.shape[0], received_ref.shape[1]
    elems = most_ref.shape[1]
    received = received_ref[...].astype(F32).reshape(slots // CAP, 2 * CAP, lanes)
    modes_t = jnp.transpose(received[:, :CAP, :].reshape(slots, lanes)).astype(BF16)
    traction = received[:, CAP:, :].reshape(slots, lanes).astype(BF16)
    inverse = 1.0 / metric_ref[0:1, :]
    copies = []
    step = 2 * LANES
    for first in range(0, elems, step):
        part = slice(first, first + step)
        wall_modes_t = mm(modes_t, elem_hot_ref[:, part]).astype(BF16)
        update = mm(wall_map_ref[...], wall_modes_t)
        new_state_ref[:, part] = (most_ref[:, part] + update * inverse[:, part]).astype(BF16)
        pair = (new_state_ref.at[:, part], new_state_hbm.at[:, part])
        copies += begin([pair], sems.at[first // step : first // step + 1])
    wall_load_ref[...] = mm(node_hot_ref[...], traction).astype(BF16)
    count = len(copies)
    copies += begin([(wall_load_ref, wall_load_hbm)], sems.at[count : count + 1])
    for copy in copies:
        copy.wait()


NEAR = pl.BlockSpec(memory_space=pltpu.VMEM)
FAR = pl.BlockSpec(memory_space=pltpu.HBM)
SCALAR = pl.BlockSpec(memory_space=pltpu.SMEM)


def call(kernel, name, outs, scratch, args, flops, specs, out_space=pltpu.VMEM, copies=0):
    size = sum(a.size * a.dtype.itemsize for a in args)
    sems = [pltpu.SemaphoreType.DMA((copies,))] if copies else []
    spec_of = {"s": SCALAR, "n": NEAR, "f": FAR}
    space_of = {"n": pltpu.VMEM, "f": pltpu.HBM}
    args = [
        pltpu.with_memory_space_constraint(a, space_of[c]) if c in space_of else a
        for a, c in zip(args, specs, strict=True)
    ]
    return pl.pallas_call(
        kernel,
        out_shape=[out_space(shape, dtype) for shape, dtype in outs],
        in_specs=[spec_of[c] for c in specs],
        out_specs=[pl.BlockSpec(memory_space=out_space)] * len(outs),
        scratch_shapes=[pltpu.VMEM(shape, dtype) for shape, dtype in scratch] + sems,
        compiler_params=pltpu.CompilerParams(vmem_limit_bytes=28 * 1024 * 1024),
        cost_estimate=pl.CostEstimate(flops=flops, bytes_accessed=size, transcendentals=0),
        name=name,
    )(*args)


def on_device(
    state,
    adjoint,
    right_side,
    source,
    metric,
    basis_tiles,
    face_tiles,
    precond,
    wall_tile,
    traction_tile,
    mode_rows,
    neighbors,
    wall_node,
    wall_target,
):
    elems, width = state.shape
    nodes, lanes = mode_rows.shape
    geo, faces = basis_tiles.shape[0], face_tiles.shape[0]
    devices = lax.axis_size("elem")
    slots = devices * CAP
    state, adjoint, right_side, source = state.T, adjoint.T, right_side.T, source.T
    neighbors = neighbors.T
    wall_node, wall_target = wall_node.reshape(1, elems), wall_target.reshape(1, nodes)
    parity = (lax.axis_index("elem") % 2).reshape(1)
    unit = 2 * elems * width * width

    def like(x):
        return (x.shape, x.dtype)

    message = ((width + 16, LANES), BF16)
    same_chip, next_chip, adjoint, neighbors = call(
        pack_kernel,
        "pack",
        [message, message, like(adjoint), like(neighbors)],
        [((width, LANES), BF16), ((width, LANES), BF16)],
        (parity, state, adjoint, neighbors),
        1000,
        "sfff",
        copies=4,
    )
    pairs = [(i, i + 1) for i in range(1, devices - 1, 2)]
    next_chip = lax.ppermute(next_chip, "elem", pairs + [(j, i) for i, j in pairs])
    pairs = [(i, i + 1) for i in range(0, devices, 2)]
    same_chip = lax.ppermute(same_chip, "elem", pairs + [(j, i) for i, j in pairs])

    (
        partial,
        inner,
        w_faces,
        traction_t,
        srow,
        out_modes,
        out_traction,
        metric,
        basis_tiles,
        face_tiles,
        precond,
    ) = call(
        inner_kernel,
        "inner",
        [
            ((width, 2 * LANES), F32),
            ((width, elems - 2 * LANES), BF16),
            ((width, faces * width), BF16),
            ((lanes, width), BF16),
            ((8, elems), F32),
            ((slots, lanes), F32),
            ((slots, lanes), F32),
            like(metric),
            like(basis_tiles),
            like(face_tiles),
            like(precond),
        ],
        [
            (((geo + faces) * width, elems), BF16),
            ((width, geo * width), BF16),
            like(source),
            like(traction_tile),
            like(mode_rows),
            like(wall_node),
            like(wall_target),
        ],
        (
            adjoint,
            neighbors,
            source,
            metric,
            basis_tiles,
            face_tiles,
            precond,
            traction_tile,
            mode_rows,
            wall_node,
            wall_target,
        ),
        (geo + faces + 3) * unit,
        "nnfffffffff",
        copies=9,
    )
    new_adjoint, send = call(
        edge_kernel,
        "edge",
        [((width, elems), BF16), ((2 * slots, lanes), BF16)],
        [((faces * width, LANES), BF16)],
        (
            parity,
            same_chip,
            next_chip,
            adjoint,
            metric,
            partial,
            inner,
            w_faces,
            precond,
            traction_t,
            srow,
            out_modes,
            out_traction,
        ),
        3 * unit,
        "snnnnnnnnnnnn",
    )
    received = lax.all_to_all(send, "elem", 0, 0, tiled=True)
    most, wall_map, elem_hot, node_hot = call(
        forward_kernel,
        "forward",
        [
            ((width, elems), F32),
            ((width, lanes), BF16),
            ((slots, elems), BF16),
            ((nodes, slots), BF16),
        ],
        [
            ((elems, (geo + faces) * width), BF16),
            (((geo + faces) * width, width), BF16),
            like(state),
            like(right_side),
            like(wall_tile.T),
            like(wall_target),
        ],
        (
            parity,
            same_chip,
            next_chip,
            metric,
            precond,
            neighbors,
            srow,
            basis_tiles,
            face_tiles,
            state,
            right_side,
            wall_tile.T,
            wall_target,
            new_adjoint,
        ),
        (geo + faces + 3) * unit,
        "snnnnnnnnffffn",
        copies=4,
    )
    new_state, wall_load = call(
        finish_kernel,
        "finish",
        [((width, elems), BF16), ((nodes, lanes), BF16)],
        [((width, elems), BF16), ((nodes, lanes), BF16)],
        (metric, most, wall_map, elem_hot, node_hot, received),
        2 * unit,
        "nnnnnn",
        out_space=pltpu.HBM,
        copies=elems // (2 * LANES) + 1,
    )
    return (new_state.T, new_adjoint.T, wall_load)


def solution(mesh):
    rows = P(("phase", "elem"), None)
    return jax.shard_map(
        on_device,
        mesh=mesh,
        in_specs=(
            rows,
            rows,
            rows,
            rows,
            P(None, "elem"),
            P("phase", None, None),
            P("phase", None, None),
            P("phase", None),
            P("phase", None),
            P("phase", None),
            rows,
            P("elem", None),
            P("elem"),
            P("elem"),
        ),
        out_specs=(rows, rows, rows),
        check_vma=False,
    )
```

```python
import jax
import jax.numpy as jnp
from jax import lax
from jax.experimental import pallas as pl
from jax.experimental.pallas import tpu as pltpu
from jax.sharding import PartitionSpec as P

HALO = 64
LANES = 128
MAIN = 256
CAP = 8
NOWHERE = -1000.0
F32 = jnp.float32
BF16 = jnp.bfloat16
NT = (((1,), (1,)), ((), ()))
TN = (((0,), (0,)), ((), ()))


def mm(left, right):
    return jnp.dot(left, right, preferred_element_type=F32)


def mm_nt(left, right):
    return lax.dot_general(left, right, NT, preferred_element_type=F32)


def mm_tn(left, right):
    return lax.dot_general(left, right, TN, preferred_element_type=F32)


def lane(rows, width=LANES):
    return lax.broadcasted_iota(jnp.int32, (rows, width), 1)


def hot(left, right):
    return jnp.where(left == right, 1.0, 0.0).astype(BF16)


def half_roll(x):
    return jnp.concatenate([x[:, HALO:], x[:, :HALO]], axis=1)


def columns_of(rows):
    fill = jnp.zeros((LANES - rows.shape[0], rows.shape[1]), F32)
    return jnp.transpose(jnp.concatenate([rows, fill], axis=0))


def transposed(x):
    m, n = x.shape
    x = x.astype(F32)
    if m % LANES:
        x = jnp.concatenate([x, jnp.zeros((LANES - m % LANES, n), F32)], axis=0)
    if n % LANES:
        x = jnp.concatenate([x, jnp.zeros((x.shape[0], LANES - n % LANES), F32)], axis=1)
    return jnp.transpose(x)[:n, :m]


def offsets(neighbors, first, elems):
    position = first + lax.broadcasted_iota(jnp.int32, neighbors.shape, 1)
    distance = ((neighbors - position + HALO) & (elems - 1)) - HALO
    return distance, neighbors >= 0, position


def padded_rows(x, rows):
    return jnp.concatenate([x, jnp.zeros((rows - x.shape[0], x.shape[1]), x.dtype)], axis=0)


def key_column(key_row):
    return jnp.transpose(jnp.broadcast_to(key_row, (LANES, key_row.shape[1])))[:, :1]


def rank_row(key_row, base_row):
    column = key_column(key_row)
    return jnp.sum(jnp.where((column < key_row) & (column >= base_row), 1.0, 0.0), axis=0, keepdims=True)


def rank_column(key_row, base_row):
    key, base = key_column(key_row), key_column(base_row)
    return jnp.sum(jnp.where((key_row < key) & (key_row >= base), 1.0, 0.0), axis=1, keepdims=True)


def node_keys(target, elems):
    nodes = target.shape[1]
    device = (target // elems).astype(F32)
    key = device * nodes + lax.broadcasted_iota(jnp.int32, (1, nodes), 1).astype(F32)
    return device, key, device * nodes


def adjoint_halo(parity, same_chip, next_chip):
    mask = (lane(same_chip.shape[0]) < HALO).astype(jnp.int32) != parity
    return jnp.where(mask, next_chip.astype(F32), same_chip.astype(F32))


def state_halo(parity, same_chip, next_chip):
    mask = (lane(same_chip.shape[0]) < HALO).astype(jnp.int32) != parity
    return jnp.where(mask, same_chip.astype(F32), next_chip.astype(F32))


def begin(copies, sems):
    started = [pltpu.make_async_copy(a, b, sems.at[i]) for i, (a, b) in enumerate(copies)]
    for copy in started:
        copy.start()
    return started


def pack_kernel(
    parity_ref,
    state_hbm,
    adjoint_hbm,
    neighbors_hbm,
    same_chip_ref,
    next_chip_ref,
    adjoint_ref,
    neighbors_ref,
    first_ref,
    last_ref,
    sems,
):
    width, elems = adjoint_ref.shape
    final = elems - LANES
    copies = begin(
        [
            (neighbors_hbm, neighbors_ref),
            (state_hbm.at[:, :LANES], first_ref),
            (state_hbm.at[:, final:], last_ref),
            (adjoint_hbm, adjoint_ref),
        ],
        sems,
    )
    low = lane(width) < HALO
    rows = same_chip_ref.shape[0] - width
    copies[0].wait()

    def codes(first):
        distance, linked, _ = offsets(neighbors_ref[:, first : first + LANES], first, elems)
        code = jnp.where(linked, distance + (HALO + 1), 0).astype(F32)
        return half_roll(padded_rows(code, rows)).astype(BF16)

    up_code, down_code = codes(final), codes(0)
    for copy in copies[1:]:
        copy.wait()

    def adjoint(first):
        return half_roll(adjoint_ref[:, first : first + LANES].astype(F32))

    up = jnp.where(low, adjoint(final), last_ref[...].astype(F32)).astype(BF16)
    down = jnp.where(low, first_ref[...].astype(F32), adjoint(0)).astype(BF16)

    @pl.when(parity_ref[0] == 0)
    def _():
        same_chip_ref[:width, :], same_chip_ref[width:, :] = up, up_code
        next_chip_ref[:width, :], next_chip_ref[width:, :] = down, down_code

    @pl.when(parity_ref[0] != 0)
    def _():
        same_chip_ref[:width, :], same_chip_ref[width:, :] = down, down_code
        next_chip_ref[:width, :], next_chip_ref[width:, :] = up, up_code


def spread(x_ref, first, count, lanes, gathered):
    for f in range(count):
        one = gathered[:, f * LANES : (f + 1) * LANES].astype(BF16)
        rest = one.shape[0] - MAIN
        x_ref[first + f * MAIN : first + (f + 1) * MAIN, lanes] = one[:MAIN, :]
        start = first + count * MAIN + f * rest
        x_ref[start : start + rest, lanes] = one[MAIN:, :]


def side_by_side(w_ref, start, tiles_ref, first, count):
    width = tiles_ref.shape[1]
    for k in range(count):
        at = start + k * MAIN
        w_ref[:, at : at + MAIN] = tiles_ref[first + k, :, :MAIN]
    w_ref[:, start + count * MAIN : start + count * width] = jnp.concatenate(
        [tiles_ref[first + k, :, MAIN:] for k in range(count)], axis=1
    )


def inner_kernel(
    adjoint_ref,
    neighbors_ref,
    source_hbm,
    metric_hbm,
    basis_hbm,
    faces_hbm,
    precond_hbm,
    traction_tile_hbm,
    mode_hbm,
    wall_node_hbm,
    wall_target_hbm,
    partial_ref,
    inner_ref,
    w_faces_ref,
    traction_t_ref,
    srow_ref,
    out_modes_ref,
    out_traction_ref,
    metric_ref,
    precond_ref,
    x_ref,
    w_ref,
    basis_ref,
    faces_ref,
    source_ref,
    traction_tile_ref,
    mode_ref,
    wall_node_ref,
    wall_target_ref,
    sems,
):
    width, elems = adjoint_ref.shape
    geo, count = basis_ref.shape[0], faces_ref.shape[0]
    tail = width - MAIN
    nodes = mode_ref.shape[0]
    half = geo // 2
    copies = begin(
        [
            (metric_hbm, metric_ref),
            (wall_node_hbm, wall_node_ref),
            (wall_target_hbm, wall_target_ref),
            (mode_hbm, mode_ref),
            (faces_hbm, faces_ref),
            (basis_hbm.at[:half], basis_ref.at[:half]),
            (source_hbm, source_ref),
            (precond_hbm, precond_ref),
            (traction_tile_hbm, traction_tile_ref),
            (basis_hbm.at[half:], basis_ref.at[half:]),
        ],
        sems,
    )

    distance, linked, position = offsets(neighbors_ref[...], 0, elems)
    target = jnp.where(linked, (position + distance).astype(F32), NOWHERE)
    span = LANES + 2 * HALO
    base = geo * width
    for b in range(elems // LANES):
        start = min(max(b * LANES - HALO, 0), elems - span)
        row = b * LANES + lax.broadcasted_iota(jnp.int32, (LANES, span), 0)
        named = jnp.concatenate(
            [hot(row.astype(F32), target[f : f + 1, start : start + span]) for f in range(count)],
            axis=0,
        )
        gathered = mm_nt(adjoint_ref[:, start : start + span], named)
        spread(x_ref, base, count, slice(b * LANES, (b + 1) * LANES), gathered)

    for copy in copies[:4]:
        copy.wait()
    value = adjoint_ref[...].astype(F32)
    for k in range(geo):
        scaled = (value * metric_ref[k : k + 1, :]).astype(BF16)
        start = k // half * half * width
        main = start + k % half * MAIN
        x_ref[main : main + MAIN, :] = scaled[:MAIN, :]
        rest = start + half * MAIN + k % half * tail
        x_ref[rest : rest + tail, :] = scaled[MAIN:, :]

    copies[4].wait()
    side_by_side(w_faces_ref, 0, faces_ref, 0, count)
    total = mm(w_faces_ref[...], x_ref[base:, :])
    middle = half * width
    copies[5].wait()
    side_by_side(w_ref, 0, basis_ref, 0, half)
    total += mm(w_ref[:, :middle], x_ref[:middle, :])
    for copy in copies[6:]:
        copy.wait()
    side_by_side(w_ref, middle, basis_ref, half, half)
    total += mm(w_ref[:, middle:], x_ref[middle:base, :])
    node = wall_node_ref[...]
    on_wall = node >= 0
    owner = jnp.where(on_wall, node // nodes, 0).astype(F32)
    elem_slot = owner * CAP + rank_row(node.astype(F32), owner * nodes)
    elem_slot = jnp.where(on_wall, elem_slot, NOWHERE)
    device, key, key_base = node_keys(wall_target_ref[...], elems)
    node_slot = device * CAP + rank_row(key, key_base)
    srow_ref[...] = jnp.zeros(srow_ref.shape, F32)
    srow_ref[0:1, :] = elem_slot
    srow_ref[1:2, :nodes] = node_slot
    slots = out_modes_ref.shape[0]
    place = lax.broadcasted_iota(jnp.int32, (slots, nodes), 0).astype(F32)
    out_modes_ref[...] = mm(hot(place, node_slot), mode_ref[...])

    rest = source_ref[...].astype(F32) - total
    last = elems - LANES
    partial_ref[:, :LANES] = rest[:, :LANES]
    partial_ref[:, LANES:] = rest[:, last:]

    update = mm(precond_ref[...], rest[:, LANES:last].astype(BF16))
    inverse = 1.0 / metric_ref[0:1, LANES:last]
    inner = (value[:, LANES:last] + update * inverse).astype(BF16)
    inner_ref[...] = inner
    traction_t = transposed(traction_tile_ref[...]).astype(BF16)
    traction_t_ref[...] = traction_t
    traction = mm(traction_t, inner).astype(BF16)

    place = lax.broadcasted_iota(jnp.int32, (slots, last - LANES), 0).astype(F32)
    out_traction_ref[...] = mm_nt(hot(place, elem_slot[:, LANES:last]), traction)


def edge_kernel(
    parity_ref,
    same_chip_ref,
    next_chip_ref,
    adjoint_ref,
    metric_ref,
    partial_ref,
    inner_ref,
    w_faces_ref,
    precond_ref,
    traction_t_ref,
    srow_ref,
    out_modes_ref,
    out_traction_ref,
    new_adjoint_ref,
    send_ref,
    x_ref,
):
    width, elems = adjoint_ref.shape
    count = w_faces_ref.shape[1] // width
    last = elems - LANES
    message = adjoint_halo(parity_ref[0], same_chip_ref[...], next_chip_ref[...])
    halo, code = message[:width, :].astype(BF16), message[width : width + 8, :]
    position = lane(8)
    shift = jnp.where(position < HALO, -(2 * HALO + 1), -1)
    target = jnp.where(code == 0.0, NOWHERE, code + (position + shift).astype(F32))
    row = lax.broadcasted_iota(jnp.int32, (LANES, LANES), 0).astype(F32)
    named = jnp.concatenate([hot(row, target[f : f + 1, :]) for f in range(count)], axis=0)
    spread(x_ref, 0, count, slice(0, LANES), mm_nt(halo, named))
    owed = mm(w_faces_ref[...], x_ref[...])
    low = lane(width) < HALO
    rest = jnp.concatenate(
        [
            partial_ref[:, :LANES] - jnp.where(low, owed, 0.0),
            partial_ref[:, LANES:] - jnp.where(low, 0.0, owed),
        ],
        axis=1,
    )
    update = mm(precond_ref[...], rest.astype(BF16))

    def ends(x):
        return jnp.concatenate([x[:, :LANES], x[:, last:]], axis=1)

    inverse = 1.0 / ends(metric_ref[0:1, :])
    edge = (ends(adjoint_ref[...]).astype(F32) + update * inverse).astype(BF16)
    new_adjoint_ref[:, :LANES] = edge[:, :LANES]
    new_adjoint_ref[:, LANES:last] = inner_ref[...]
    new_adjoint_ref[:, last:] = edge[:, LANES:]
    traction = mm(traction_t_ref[...], edge).astype(BF16)
    slots, lanes = out_modes_ref.shape
    place = lax.broadcasted_iota(jnp.int32, (slots, 2 * LANES), 0).astype(F32)
    out_traction = out_traction_ref[...] + mm_nt(hot(place, ends(srow_ref[0:1, :])), traction)
    both = [x.reshape(slots // CAP, CAP, lanes) for x in (out_modes_ref[...], out_traction)]
    send_ref[...] = jnp.concatenate(both, axis=1).reshape(2 * slots, lanes).astype(BF16)


def forward_kernel(
    parity_ref,
    same_chip_ref,
    next_chip_ref,
    metric_ref,
    precond_ref,
    neighbors_ref,
    srow_ref,
    basis_hbm,
    faces_hbm,
    state_hbm,
    right_hbm,
    wall_tile_t_hbm,
    wall_target_hbm,
    after_hbm,
    most_ref,
    wall_map_ref,
    elem_hot_ref,
    node_hot_ref,
    x_ref,
    w_ref,
    basis_ref,
    faces_ref,
    state_ref,
    right_ref,
    wall_tile_t_ref,
    wall_target_ref,
    sems,
):
    width, elems = state_ref.shape
    copies = begin(
        [
            (state_hbm, state_ref),
            (right_hbm, right_ref),
            (wall_tile_t_hbm, wall_tile_t_ref),
            (wall_target_hbm, wall_target_ref),
            (faces_hbm, faces_ref),
            (basis_hbm, basis_ref),
        ],
        sems,
    )
    copies[0].wait()
    geo, count = basis_ref.shape[0], faces_ref.shape[0]
    tail = width - MAIN
    base = geo * width
    factors = columns_of(metric_ref[...])
    value = transposed(state_ref[...])
    tails = []
    for k in range(geo):
        scaled = (value * factors[:, k : k + 1]).astype(BF16)
        x_ref[:, k * MAIN : (k + 1) * MAIN] = scaled[:, :MAIN]
        tails.append(scaled[:, MAIN:])
    x_ref[:, geo * MAIN : base] = jnp.concatenate(tails, axis=1)

    distance, linked, position = offsets(neighbors_ref[...], 0, elems)
    source = position + distance
    span = LANES + 2 * HALO
    last = elems - LANES
    block = position // LANES
    shift = jnp.where(
        position < LANES,
        jnp.where(source < 0, span, 0),
        jnp.where(
            position >= last,
            jnp.where(source >= elems, -elems, span - elems),
            HALO - block * LANES,
        ),
    )
    column = columns_of(padded_rows(jnp.where(linked, (source + shift).astype(F32), NOWHERE), 8))
    halo = state_halo(parity_ref[0], same_chip_ref[...], next_chip_ref[...])[:width, :].astype(BF16)
    place = lane(LANES, span).astype(F32)
    for b in range(elems // LANES):
        if b == 0:
            beside = jnp.concatenate([state_ref[:, : span - HALO], halo[:, HALO:]], axis=1)
        elif b == elems // LANES - 1:
            beside = jnp.concatenate([halo[:, :HALO], state_ref[:, elems - span + HALO :]], axis=1)
        else:
            beside = state_ref[:, b * LANES - HALO : b * LANES - HALO + span]
        rows = slice(b * LANES, (b + 1) * LANES)
        named = jnp.concatenate([hot(place, column[rows, f : f + 1]) for f in range(count)], axis=0)
        gathered = mm_nt(named, beside).astype(BF16)
        tails = []
        for f in range(count):
            one = gathered[f * LANES : (f + 1) * LANES, :]
            x_ref[rows, base + f * MAIN : base + (f + 1) * MAIN] = one[:, :MAIN]
            tails.append(one[:, MAIN:])
        x_ref[rows, base + count * MAIN :] = jnp.concatenate(tails, axis=1)

    for copy in copies[1:]:
        copy.wait()
    for first, tiles_ref in ((0, basis_ref), (base, faces_ref)):
        number = tiles_ref.shape[0]
        for k in range(number):
            w_ref[first + k * MAIN : first + (k + 1) * MAIN, :] = tiles_ref[k, :MAIN, :]
            start = first + number * MAIN + k * tail
            w_ref[start : start + tail, :] = tiles_ref[k, MAIN:, :]
    applied = mm(x_ref[...], w_ref[...])
    rest = (right_ref[...].astype(F32) - transposed(applied)).astype(BF16)

    precond_t = transposed(precond_ref[...]).astype(BF16)
    inverse = 1.0 / metric_ref[0:1, :]
    most_ref[...] = state_ref[...].astype(F32) + mm(precond_t, rest) * inverse
    wall_map_ref[...] = mm(precond_t, wall_tile_t_ref[...]).astype(BF16)
    slots = elem_hot_ref.shape[0]
    nodes = node_hot_ref.shape[0]
    place = lax.broadcasted_iota(jnp.int32, (slots, elems), 0).astype(F32)
    elem_hot_ref[...] = hot(place, srow_ref[0:1, :])
    device, key, key_base = node_keys(wall_target_ref[...], elems)
    node_slot = key_column(device) * CAP + rank_column(key, key_base)
    node_hot_ref[...] = hot(lane(nodes, slots).astype(F32), node_slot)


def finish_kernel(
    metric_ref,
    most_ref,
    wall_map_ref,
    elem_hot_ref,
    node_hot_ref,
    received_ref,
    new_state_hbm,
    wall_load_hbm,
    new_state_ref,
    wall_load_ref,
    sems,
):
    slots, lanes = elem_hot_ref.shape[0], received_ref.shape[1]
    elems = most_ref.shape[1]
    received = received_ref[...].astype(F32).reshape(slots // CAP, 2 * CAP, lanes)
    modes = received[:, :CAP, :].reshape(slots, lanes).astype(BF16)
    traction = received[:, CAP:, :].reshape(slots, lanes).astype(BF16)
    inverse = 1.0 / metric_ref[0:1, :]
    copies = []
    step = 2 * LANES
    for first in range(0, elems, step):
        part = slice(first, first + step)
        wall_modes_t = mm_tn(modes, elem_hot_ref[:, part]).astype(BF16)
        update = mm(wall_map_ref[...], wall_modes_t)
        new_state_ref[:, part] = (most_ref[:, part] + update * inverse[:, part]).astype(BF16)
        pair = (new_state_ref.at[:, part], new_state_hbm.at[:, part])
        copies += begin([pair], sems.at[first // step : first // step + 1])
    wall_load_ref[...] = mm(node_hot_ref[...], traction).astype(BF16)
    count = len(copies)
    copies += begin([(wall_load_ref, wall_load_hbm)], sems.at[count : count + 1])
    for copy in copies:
        copy.wait()


NEAR = pl.BlockSpec(memory_space=pltpu.VMEM)
FAR = pl.BlockSpec(memory_space=pltpu.HBM)
SCALAR = pl.BlockSpec(memory_space=pltpu.SMEM)


def call(kernel, name, outs, scratch, args, flops, specs, out_space=pltpu.VMEM, copies=0):
    size = sum(a.size * a.dtype.itemsize for a in args)
    sems = [pltpu.SemaphoreType.DMA((copies,))] if copies else []
    spec_of = {"s": SCALAR, "n": NEAR, "f": FAR}
    space_of = {"n": pltpu.VMEM, "f": pltpu.HBM}
    args = [
        pltpu.with_memory_space_constraint(a, space_of[c]) if c in space_of else a
        for a, c in zip(args, specs, strict=True)
    ]
    return pl.pallas_call(
        kernel,
        out_shape=[out_space(shape, dtype) for shape, dtype in outs],
        in_specs=[spec_of[c] for c in specs],
        out_specs=[pl.BlockSpec(memory_space=out_space)] * len(outs),
        scratch_shapes=[pltpu.VMEM(shape, dtype) for shape, dtype in scratch] + sems,
        compiler_params=pltpu.CompilerParams(vmem_limit_bytes=28 * 1024 * 1024),
        cost_estimate=pl.CostEstimate(flops=flops, bytes_accessed=size, transcendentals=0),
        name=name,
    )(*args)


def on_device(
    state,
    adjoint,
    right_side,
    source,
    metric,
    basis_tiles,
    face_tiles,
    precond,
    wall_tile,
    traction_tile,
    mode_rows,
    neighbors,
    wall_node,
    wall_target,
):
    elems, width = state.shape
    nodes, lanes = mode_rows.shape
    geo, faces = basis_tiles.shape[0], face_tiles.shape[0]
    devices = lax.axis_size("elem")
    slots = devices * CAP
    state, adjoint, right_side, source = state.T, adjoint.T, right_side.T, source.T
    neighbors = neighbors.T
    wall_node, wall_target = wall_node.reshape(1, elems), wall_target.reshape(1, nodes)
    parity = (lax.axis_index("elem") % 2).reshape(1)
    unit = 2 * elems * width * width

    def like(x):
        return (x.shape, x.dtype)

    message = ((width + 16, LANES), BF16)
    same_chip, next_chip, adjoint, neighbors = call(
        pack_kernel,
        "pack",
        [message, message, like(adjoint), like(neighbors)],
        [((width, LANES), BF16), ((width, LANES), BF16)],
        (parity, state, adjoint, neighbors),
        1000,
        "sfff",
        copies=4,
    )
    pairs = [(i, i + 1) for i in range(1, devices - 1, 2)]
    next_chip = lax.ppermute(next_chip, "elem", pairs + [(j, i) for i, j in pairs])
    pairs = [(i, i + 1) for i in range(0, devices, 2)]
    same_chip = lax.ppermute(same_chip, "elem", pairs + [(j, i) for i, j in pairs])

    (
        partial,
        inner,
        w_faces,
        traction_t,
        srow,
        out_modes,
        out_traction,
        metric,
        precond,
    ) = call(
        inner_kernel,
        "inner",
        [
            ((width, 2 * LANES), F32),
            ((width, elems - 2 * LANES), BF16),
            ((width, faces * width), BF16),
            ((lanes, width), BF16),
            ((8, elems), F32),
            ((slots, lanes), F32),
            ((slots, lanes), F32),
            like(metric),
            like(precond),
        ],
        [
            (((geo + faces) * width, elems), BF16),
            ((width, geo * width), BF16),
            like(basis_tiles),
            like(face_tiles),
            like(source),
            like(traction_tile),
            like(mode_rows),
            like(wall_node),
            like(wall_target),
        ],
        (
            adjoint,
            neighbors,
            source,
            metric,
            basis_tiles,
            face_tiles,
            precond,
            traction_tile,
            mode_rows,
            wall_node,
            wall_target,
        ),
        (geo + faces + 3) * unit,
        "nnfffffffff",
        copies=10,
    )
    new_adjoint, send = call(
        edge_kernel,
        "edge",
        [((width, elems), BF16), ((2 * slots, lanes), BF16)],
        [((faces * width, LANES), BF16)],
        (
            parity,
            same_chip,
            next_chip,
            adjoint,
            metric,
            partial,
            inner,
            w_faces,
            precond,
            traction_t,
            srow,
            out_modes,
            out_traction,
        ),
        3 * unit,
        "snnnnnnnnnnnn",
    )
    received = lax.all_to_all(send, "elem", 0, 0, tiled=True)
    most, wall_map, elem_hot, node_hot = call(
        forward_kernel,
        "forward",
        [
            ((width, elems), F32),
            ((width, lanes), BF16),
            ((slots, elems), BF16),
            ((nodes, slots), BF16),
        ],
        [
            ((elems, (geo + faces) * width), BF16),
            (((geo + faces) * width, width), BF16),
            like(basis_tiles),
            like(face_tiles),
            like(state),
            like(right_side),
            like(wall_tile.T),
            like(wall_target),
        ],
        (
            parity,
            same_chip,
            next_chip,
            metric,
            precond,
            neighbors,
            srow,
            basis_tiles,
            face_tiles,
            state,
            right_side,
            wall_tile.T,
            wall_target,
            new_adjoint,
        ),
        (geo + faces + 3) * unit,
        "snnnnnnffffffn",
        copies=6,
    )
    new_state, wall_load = call(
        finish_kernel,
        "finish",
        [((width, elems), BF16), ((nodes, lanes), BF16)],
        [((width, elems), BF16), ((nodes, lanes), BF16)],
        (metric, most, wall_map, elem_hot, node_hot, received),
        2 * unit,
        "nnnnnn",
        out_space=pltpu.HBM,
        copies=elems // (2 * LANES) + 1,
    )
    return (new_state.T, new_adjoint.T, wall_load)


def solution(mesh):
    rows = P(("phase", "elem"), None)
    return jax.shard_map(
        on_device,
        mesh=mesh,
        in_specs=(
            rows,
            rows,
            rows,
            rows,
            P(None, "elem"),
            P("phase", None, None),
            P("phase", None, None),
            P("phase", None),
            P("phase", None),
            P("phase", None),
            rows,
            P("elem", None),
            P("elem"),
            P("elem"),
        ),
        out_specs=(rows, rows, rows),
        check_vma=False,
    )
```

```python
import jax
import jax.numpy as jnp
from jax import lax
from jax.experimental import pallas as pl
from jax.experimental.pallas import tpu as pltpu
from jax.sharding import PartitionSpec as P

HALO = 64
LANES = 128
MAIN = 256
CAP = 8
NOWHERE = -1000.0
F32 = jnp.float32
BF16 = jnp.bfloat16
NT = (((1,), (1,)), ((), ()))
TN = (((0,), (0,)), ((), ()))


def mm(left, right):
    return jnp.dot(left, right, preferred_element_type=F32)


def mm_nt(left, right):
    return lax.dot_general(left, right, NT, preferred_element_type=F32)


def mm_tn(left, right):
    return lax.dot_general(left, right, TN, preferred_element_type=F32)


def lane(rows, width=LANES):
    return lax.broadcasted_iota(jnp.int32, (rows, width), 1)


def hot(left, right):
    return jnp.where(left == right, 1.0, 0.0).astype(BF16)


def half_roll(x):
    return jnp.concatenate([x[:, HALO:], x[:, :HALO]], axis=1)


def columns_of(rows):
    fill = jnp.zeros((LANES - rows.shape[0], rows.shape[1]), F32)
    return jnp.transpose(jnp.concatenate([rows, fill], axis=0))


def transposed(x):
    m, n = x.shape
    x = x.astype(F32)
    if m % LANES:
        x = jnp.concatenate([x, jnp.zeros((LANES - m % LANES, n), F32)], axis=0)
    if n % LANES:
        x = jnp.concatenate([x, jnp.zeros((x.shape[0], LANES - n % LANES), F32)], axis=1)
    return jnp.transpose(x)[:n, :m]


def offsets(neighbors, first, elems):
    position = first + lax.broadcasted_iota(jnp.int32, neighbors.shape, 1)
    distance = ((neighbors - position + HALO) & (elems - 1)) - HALO
    return distance, neighbors >= 0, position


def padded_rows(x, rows):
    return jnp.concatenate([x, jnp.zeros((rows - x.shape[0], x.shape[1]), x.dtype)], axis=0)


def key_column(key_row):
    return jnp.transpose(jnp.broadcast_to(key_row, (LANES, key_row.shape[1])))[:, :1]


def rank_row(key_row, base_row):
    column = key_column(key_row)
    return jnp.sum(jnp.where((column < key_row) & (column >= base_row), 1.0, 0.0), axis=0, keepdims=True)


def rank_column(key_row, base_row):
    key, base = key_column(key_row), key_column(base_row)
    return jnp.sum(jnp.where((key_row < key) & (key_row >= base), 1.0, 0.0), axis=1, keepdims=True)


def node_keys(target, elems):
    nodes = target.shape[1]
    device = (target // elems).astype(F32)
    key = device * nodes + lax.broadcasted_iota(jnp.int32, (1, nodes), 1).astype(F32)
    return device, key, device * nodes


def adjoint_halo(parity, same_chip, next_chip):
    mask = (lane(same_chip.shape[0]) < HALO).astype(jnp.int32) != parity
    return jnp.where(mask, next_chip.astype(F32), same_chip.astype(F32))


def state_halo(parity, same_chip, next_chip):
    mask = (lane(same_chip.shape[0]) < HALO).astype(jnp.int32) != parity
    return jnp.where(mask, same_chip.astype(F32), next_chip.astype(F32))


def begin(copies, sems):
    started = [pltpu.make_async_copy(a, b, sems.at[i]) for i, (a, b) in enumerate(copies)]
    for copy in started:
        copy.start()
    return started


def load_kernel(
    state_hbm, adjoint_hbm, neighbors_hbm, state_ends_ref, adjoint_ends_ref, neighbors_ref, sems
):
    last = state_hbm.shape[1] - LANES
    pairs = [(neighbors_hbm, neighbors_ref)]
    for far, near in ((state_hbm, state_ends_ref), (adjoint_hbm, adjoint_ends_ref)):
        pairs.append((far.at[:, :LANES], near.at[:, :LANES]))
        pairs.append((far.at[:, last:], near.at[:, LANES:]))
    for copy in begin(pairs, sems):
        copy.wait()


def pack_kernel(
    parity_ref, state_ends_ref, adjoint_ends_ref, neighbors_ref, same_chip_ref, next_chip_ref
):
    width, elems = adjoint_ends_ref.shape[0], neighbors_ref.shape[1]
    final = elems - LANES
    low = lane(width) < HALO
    rows = same_chip_ref.shape[0] - width

    def codes(first):
        distance, linked, _ = offsets(neighbors_ref[:, first : first + LANES], first, elems)
        code = jnp.where(linked, distance + (HALO + 1), 0).astype(F32)
        return half_roll(padded_rows(code, rows)).astype(BF16)

    def adjoint(first):
        return half_roll(adjoint_ends_ref[:, first : first + LANES].astype(F32))

    up_code, down_code = codes(final), codes(0)
    up = jnp.where(low, adjoint(LANES), state_ends_ref[:, LANES:].astype(F32)).astype(BF16)
    down = jnp.where(low, state_ends_ref[:, :LANES].astype(F32), adjoint(0)).astype(BF16)

    @pl.when(parity_ref[0] == 0)
    def _():
        same_chip_ref[:width, :], same_chip_ref[width:, :] = up, up_code
        next_chip_ref[:width, :], next_chip_ref[width:, :] = down, down_code

    @pl.when(parity_ref[0] != 0)
    def _():
        same_chip_ref[:width, :], same_chip_ref[width:, :] = down, down_code
        next_chip_ref[:width, :], next_chip_ref[width:, :] = up, up_code


def spread(x_ref, first, count, lanes, gathered):
    for f in range(count):
        one = gathered[:, f * LANES : (f + 1) * LANES].astype(BF16)
        rest = one.shape[0] - MAIN
        x_ref[first + f * MAIN : first + (f + 1) * MAIN, lanes] = one[:MAIN, :]
        start = first + count * MAIN + f * rest
        x_ref[start : start + rest, lanes] = one[MAIN:, :]


def side_by_side(w_ref, tiles_ref):
    count, width, _ = tiles_ref.shape
    for k in range(count):
        w_ref[:, k * MAIN : (k + 1) * MAIN] = tiles_ref[k, :, :MAIN]
    w_ref[:, count * MAIN :] = jnp.concatenate(
        [tiles_ref[k, :, MAIN:] for k in range(count)], axis=1
    )


def inner_kernel(
    adjoint_ref,
    neighbors_ref,
    source_ref,
    metric_ref,
    basis_ref,
    faces_ref,
    precond_ref,
    traction_tile_ref,
    mode_ref,
    wall_node_ref,
    wall_target_ref,
    partial_ref,
    inner_ref,
    w_faces_ref,
    maps_ref,
    edge_traction_ref,
    edge_inverse_ref,
    edge_hot_ref,
    srow_ref,
    out_modes_ref,
    out_traction_ref,
    metric_out_ref,
    precond_out_ref,
    x_ref,
    w_ref,
):
    width, elems = adjoint_ref.shape
    geo, count = basis_ref.shape[0], faces_ref.shape[0]
    tail = width - MAIN
    nodes, lanes = mode_ref.shape
    distance, linked, position = offsets(neighbors_ref[...], 0, elems)
    target = jnp.where(linked, (position + distance).astype(F32), NOWHERE)
    span = LANES + 2 * HALO
    base = geo * width
    for b in range(elems // LANES):
        start = min(max(b * LANES - HALO, 0), elems - span)
        row = b * LANES + lax.broadcasted_iota(jnp.int32, (LANES, span), 0)
        named = jnp.concatenate(
            [hot(row.astype(F32), target[f : f + 1, start : start + span]) for f in range(count)],
            axis=0,
        )
        gathered = mm_nt(adjoint_ref[:, start : start + span], named)
        spread(x_ref, base, count, slice(b * LANES, (b + 1) * LANES), gathered)

    value = adjoint_ref[...].astype(F32)
    for k in range(geo):
        scaled = (value * metric_ref[k : k + 1, :]).astype(BF16)
        x_ref[k * MAIN : (k + 1) * MAIN, :] = scaled[:MAIN, :]
        start = geo * MAIN + k * tail
        x_ref[start : start + tail, :] = scaled[MAIN:, :]
    side_by_side(w_faces_ref, faces_ref)
    total = mm(w_faces_ref[...], x_ref[base:, :])
    side_by_side(w_ref, basis_ref)
    total += mm(w_ref[...], x_ref[:base, :])
    metric_out_ref[...] = metric_ref[...]
    precond_out_ref[...] = precond_ref[...]

    node = wall_node_ref[...]
    on_wall = node >= 0
    owner = jnp.where(on_wall, node // nodes, 0).astype(F32)
    elem_slot = owner * CAP + rank_row(node.astype(F32), owner * nodes)
    elem_slot = jnp.where(on_wall, elem_slot, NOWHERE)
    device, key, key_base = node_keys(wall_target_ref[...], elems)
    node_slot = device * CAP + rank_row(key, key_base)
    srow_ref[...] = jnp.zeros(srow_ref.shape, F32)
    srow_ref[0:1, :] = elem_slot
    srow_ref[1:2, :nodes] = node_slot
    slots = out_modes_ref.shape[0]
    place = lax.broadcasted_iota(jnp.int32, (slots, nodes), 0).astype(F32)
    out_modes_ref[...] = mm(hot(place, node_slot), mode_ref[...])

    rest = source_ref[...].astype(F32) - total
    last = elems - LANES
    partial_ref[:, :LANES] = rest[:, :LANES]
    partial_ref[:, LANES:] = rest[:, last:]

    traction_t = transposed(traction_tile_ref[...]).astype(BF16)
    maps_ref[:width, :] = precond_ref[...]
    both = mm(traction_t, precond_ref[...])
    coarse = both.astype(BF16)
    maps_ref[width : width + lanes, :] = coarse
    maps_ref[width + lanes :, :] = (both - coarse.astype(F32)).astype(BF16)
    edge_traction_ref[:, :LANES] = mm(traction_t, adjoint_ref[:, :LANES])
    edge_traction_ref[:, LANES:] = mm(traction_t, adjoint_ref[:, last:])
    update = mm(precond_ref[...], rest[:, LANES:last].astype(BF16))
    inverse = 1.0 / metric_ref[0:1, :]
    edge_inverse_ref[...] = jnp.concatenate([inverse[:, :LANES], inverse[:, last:]], axis=1)
    inner = (value[:, LANES:last] + update * inverse[:, LANES:last]).astype(BF16)
    inner_ref[...] = inner
    traction = mm(traction_t, inner).astype(BF16)

    place = lax.broadcasted_iota(jnp.int32, (slots, last - LANES), 0).astype(F32)
    out_traction_ref[...] = mm_nt(hot(place, elem_slot[:, LANES:last]), traction)
    edge_slot = jnp.concatenate([elem_slot[:, :LANES], elem_slot[:, last:]], axis=1)
    edge_hot_ref[...] = hot(place, edge_slot)


def edge_kernel(
    parity_ref,
    next_chip_ref,
    same_chip_ref,
    adjoint_ends_ref,
    partial_ref,
    inner_ref,
    w_faces_ref,
    maps_ref,
    edge_traction_ref,
    edge_inverse_ref,
    edge_hot_ref,
    out_modes_ref,
    out_traction_ref,
    new_adjoint_ref,
    send_ref,
    x_ref,
):
    width, elems = new_adjoint_ref.shape
    count = w_faces_ref.shape[1] // width
    last = elems - LANES
    slots, lanes = out_modes_ref.shape
    message = adjoint_halo(parity_ref[0], same_chip_ref[...], next_chip_ref[...])
    halo, code = message[:width, :].astype(BF16), message[width : width + 8, :]
    position = lane(8)
    shift = jnp.where(position < HALO, -(2 * HALO + 1), -1)
    target = jnp.where(code == 0.0, NOWHERE, code + (position + shift).astype(F32))
    row = lax.broadcasted_iota(jnp.int32, (LANES, LANES), 0).astype(F32)
    named = jnp.concatenate([hot(row, target[f : f + 1, :]) for f in range(count)], axis=0)
    spread(x_ref, 0, count, slice(0, LANES), mm_nt(halo, named))
    owed = mm(w_faces_ref[...], x_ref[...])
    low = lane(width) < HALO
    rest = jnp.concatenate(
        [
            partial_ref[:, :LANES] - jnp.where(low, owed, 0.0),
            partial_ref[:, LANES:] - jnp.where(low, 0.0, owed),
        ],
        axis=1,
    )
    update = mm(maps_ref[...], rest.astype(BF16)) * edge_inverse_ref[...]
    fine = update[width : width + lanes, :] + update[width + lanes :, :]
    traction = (edge_traction_ref[...] + fine).astype(BF16)
    out_traction = out_traction_ref[...] + mm_nt(edge_hot_ref[...], traction)
    both = [x.reshape(slots // CAP, CAP, lanes) for x in (out_modes_ref[...], out_traction)]
    send_ref[...] = jnp.concatenate(both, axis=1).reshape(2 * slots, lanes).astype(BF16)
    edge = (adjoint_ends_ref[...].astype(F32) + update[:width, :]).astype(BF16)
    new_adjoint_ref[:, :LANES] = edge[:, :LANES]
    new_adjoint_ref[:, LANES:last] = inner_ref[...]
    new_adjoint_ref[:, last:] = edge[:, LANES:]


def forward_kernel(
    parity_ref,
    next_chip_ref,
    same_chip_ref,
    metric_ref,
    precond_ref,
    neighbors_ref,
    srow_ref,
    basis_hbm,
    faces_hbm,
    state_hbm,
    right_hbm,
    wall_tile_t_hbm,
    wall_target_hbm,
    after_hbm,
    most_ref,
    wall_map_ref,
    elem_hot_ref,
    node_hot_ref,
    x_ref,
    w_ref,
    basis_ref,
    faces_ref,
    state_ref,
    right_ref,
    wall_tile_t_ref,
    wall_target_ref,
    sems,
):
    width, elems = state_ref.shape
    copies = begin(
        [
            (state_hbm, state_ref),
            (right_hbm, right_ref),
            (wall_tile_t_hbm, wall_tile_t_ref),
            (wall_target_hbm, wall_target_ref),
            (faces_hbm, faces_ref),
            (basis_hbm, basis_ref),
        ],
        sems,
    )
    copies[0].wait()
    geo, count = basis_ref.shape[0], faces_ref.shape[0]
    tail = width - MAIN
    base = geo * width
    factors = columns_of(metric_ref[...])
    value = transposed(state_ref[...])
    tails = []
    for k in range(geo):
        scaled = (value * factors[:, k : k + 1]).astype(BF16)
        x_ref[:, k * MAIN : (k + 1) * MAIN] = scaled[:, :MAIN]
        tails.append(scaled[:, MAIN:])
    x_ref[:, geo * MAIN : base] = jnp.concatenate(tails, axis=1)

    distance, linked, position = offsets(neighbors_ref[...], 0, elems)
    source = position + distance
    span = LANES + 2 * HALO
    last = elems - LANES
    block = position // LANES
    shift = jnp.where(
        position < LANES,
        jnp.where(source < 0, span, 0),
        jnp.where(
            position >= last,
            jnp.where(source >= elems, -elems, span - elems),
            HALO - block * LANES,
        ),
    )
    column = columns_of(padded_rows(jnp.where(linked, (source + shift).astype(F32), NOWHERE), 8))
    halo = state_halo(parity_ref[0], same_chip_ref[...], next_chip_ref[...])[:width, :].astype(BF16)
    place = lane(LANES, span).astype(F32)
    for b in range(elems // LANES):
        if b == 0:
            beside = jnp.concatenate([state_ref[:, : span - HALO], halo[:, HALO:]], axis=1)
        elif b == elems // LANES - 1:
            beside = jnp.concatenate([halo[:, :HALO], state_ref[:, elems - span + HALO :]], axis=1)
        else:
            beside = state_ref[:, b * LANES - HALO : b * LANES - HALO + span]
        rows = slice(b * LANES, (b + 1) * LANES)
        named = jnp.concatenate([hot(place, column[rows, f : f + 1]) for f in range(count)], axis=0)
        gathered = mm_nt(named, beside).astype(BF16)
        tails = []
        for f in range(count):
            one = gathered[f * LANES : (f + 1) * LANES, :]
            x_ref[rows, base + f * MAIN : base + (f + 1) * MAIN] = one[:, :MAIN]
            tails.append(one[:, MAIN:])
        x_ref[rows, base + count * MAIN :] = jnp.concatenate(tails, axis=1)

    for copy in copies[1:]:
        copy.wait()
    for first, tiles_ref in ((0, basis_ref), (base, faces_ref)):
        number = tiles_ref.shape[0]
        for k in range(number):
            w_ref[first + k * MAIN : first + (k + 1) * MAIN, :] = tiles_ref[k, :MAIN, :]
            start = first + number * MAIN + k * tail
            w_ref[start : start + tail, :] = tiles_ref[k, MAIN:, :]
    applied = mm(x_ref[...], w_ref[...])
    rest = (right_ref[...].astype(F32) - transposed(applied)).astype(BF16)

    precond_t = transposed(precond_ref[...]).astype(BF16)
    inverse = 1.0 / metric_ref[0:1, :]
    most_ref[...] = state_ref[...].astype(F32) + mm(precond_t, rest) * inverse
    wall_map_ref[...] = mm(precond_t, wall_tile_t_ref[...]).astype(BF16)
    slots = elem_hot_ref.shape[0]
    nodes = node_hot_ref.shape[0]
    place = lax.broadcasted_iota(jnp.int32, (slots, elems), 0).astype(F32)
    elem_hot_ref[...] = hot(place, srow_ref[0:1, :])
    device, key, key_base = node_keys(wall_target_ref[...], elems)
    node_slot = key_column(device) * CAP + rank_column(key, key_base)
    node_hot_ref[...] = hot(lane(nodes, slots).astype(F32), node_slot)


def finish_kernel(
    metric_ref,
    most_ref,
    wall_map_ref,
    elem_hot_ref,
    node_hot_ref,
    received_ref,
    new_state_hbm,
    wall_load_hbm,
    new_state_ref,
    wall_load_ref,
    sems,
):
    slots, lanes = elem_hot_ref.shape[0], received_ref.shape[1]
    elems = most_ref.shape[1]
    received = received_ref[...].astype(F32).reshape(slots // CAP, 2 * CAP, lanes)
    modes = received[:, :CAP, :].reshape(slots, lanes).astype(BF16)
    traction = received[:, CAP:, :].reshape(slots, lanes).astype(BF16)
    inverse = 1.0 / metric_ref[0:1, :]
    copies = []
    step = 2 * LANES
    for first in range(0, elems, step):
        part = slice(first, first + step)
        wall_modes_t = mm_tn(modes, elem_hot_ref[:, part]).astype(BF16)
        update = mm(wall_map_ref[...], wall_modes_t)
        new_state_ref[:, part] = (most_ref[:, part] + update * inverse[:, part]).astype(BF16)
        pair = (new_state_ref.at[:, part], new_state_hbm.at[:, part])
        copies += begin([pair], sems.at[first // step : first // step + 1])
    wall_load_ref[...] = mm(node_hot_ref[...], traction).astype(BF16)
    count = len(copies)
    copies += begin([(wall_load_ref, wall_load_hbm)], sems.at[count : count + 1])
    for copy in copies:
        copy.wait()


NEAR = pl.BlockSpec(memory_space=pltpu.VMEM)
FAR = pl.BlockSpec(memory_space=pltpu.HBM)
SCALAR = pl.BlockSpec(memory_space=pltpu.SMEM)


def call(kernel, name, outs, scratch, args, flops, specs, out_space=pltpu.VMEM, copies=0):
    size = sum(a.size * a.dtype.itemsize for a in args)
    sems = [pltpu.SemaphoreType.DMA((copies,))] if copies else []
    spec_of = {"s": SCALAR, "n": NEAR, "f": FAR}
    space_of = {"n": pltpu.VMEM, "f": pltpu.HBM}
    args = [
        pltpu.with_memory_space_constraint(a, space_of[c]) if c in space_of else a
        for a, c in zip(args, specs, strict=True)
    ]
    return pl.pallas_call(
        kernel,
        out_shape=[out_space(shape, dtype) for shape, dtype in outs],
        in_specs=[spec_of[c] for c in specs],
        out_specs=[pl.BlockSpec(memory_space=out_space)] * len(outs),
        scratch_shapes=[pltpu.VMEM(shape, dtype) for shape, dtype in scratch] + sems,
        compiler_params=pltpu.CompilerParams(vmem_limit_bytes=28 * 1024 * 1024),
        cost_estimate=pl.CostEstimate(flops=flops, bytes_accessed=size, transcendentals=0),
        name=name,
    )(*args)


def on_device(
    state,
    adjoint,
    right_side,
    source,
    metric,
    basis_tiles,
    face_tiles,
    precond,
    wall_tile,
    traction_tile,
    mode_rows,
    neighbors,
    wall_node,
    wall_target,
):
    elems, width = state.shape
    nodes, lanes = mode_rows.shape
    geo, faces = basis_tiles.shape[0], face_tiles.shape[0]
    devices = lax.axis_size("elem")
    slots = devices * CAP
    state, adjoint, right_side, source = state.T, adjoint.T, right_side.T, source.T
    neighbors = neighbors.T
    wall_node, wall_target = wall_node.reshape(1, elems), wall_target.reshape(1, nodes)
    parity = (lax.axis_index("elem") % 2).reshape(1)
    unit = 2 * elems * width * width

    def like(x):
        return (x.shape, x.dtype)

    message = ((width + 16, LANES), BF16)
    ends = ((width, 2 * LANES), BF16)
    state_ends, adjoint_ends, neighbors = call(
        load_kernel,
        "load",
        [ends, ends, like(neighbors)],
        [],
        (state, adjoint, neighbors),
        1000,
        "fff",
        copies=5,
    )
    same_chip, next_chip = call(
        pack_kernel,
        "pack",
        [message, message],
        [],
        (parity, state_ends, adjoint_ends, neighbors),
        10**10,
        "snnn",
    )
    pairs = [(i, i + 1) for i in range(1, devices - 1, 2)]
    next_chip = lax.ppermute(next_chip, "elem", pairs + [(j, i) for i, j in pairs])
    pairs = [(i, i + 1) for i in range(0, devices, 2)]
    same_chip = lax.ppermute(same_chip, "elem", pairs + [(j, i) for i, j in pairs])

    (
        partial,
        inner,
        w_faces,
        maps,
        edge_traction,
        edge_inverse,
        edge_hot,
        srow,
        out_modes,
        out_traction,
        metric,
        precond,
    ) = call(
        inner_kernel,
        "inner",
        [
            ((width, 2 * LANES), F32),
            ((width, elems - 2 * LANES), BF16),
            ((width, faces * width), BF16),
            ((width + 2 * lanes, width), BF16),
            ((lanes, 2 * LANES), F32),
            ((1, 2 * LANES), F32),
            ((slots, 2 * LANES), BF16),
            ((8, elems), F32),
            ((slots, lanes), F32),
            ((slots, lanes), F32),
            like(metric),
            like(precond),
        ],
        [
            (((geo + faces) * width, elems), BF16),
            ((width, geo * width), BF16),
        ],
        (
            adjoint,
            neighbors,
            source,
            metric,
            basis_tiles,
            face_tiles,
            precond,
            traction_tile,
            mode_rows,
            wall_node,
            wall_target,
        ),
        (geo + faces + 3) * unit,
        "nnnnnnnnnnn",
    )
    new_adjoint, send = call(
        edge_kernel,
        "edge",
        [((width, elems), BF16), ((2 * slots, lanes), BF16)],
        [((faces * width, LANES), BF16)],
        (
            parity,
            next_chip,
            same_chip,
            adjoint_ends,
            partial,
            inner,
            w_faces,
            maps,
            edge_traction,
            edge_inverse,
            edge_hot,
            out_modes,
            out_traction,
        ),
        3 * unit,
        "snnnnnnnnnnnn",
    )
    received = lax.all_to_all(send, "elem", 0, 0, tiled=True)
    most, wall_map, elem_hot, node_hot = call(
        forward_kernel,
        "forward",
        [
            ((width, elems), F32),
            ((width, lanes), BF16),
            ((slots, elems), BF16),
            ((nodes, slots), BF16),
        ],
        [
            ((elems, (geo + faces) * width), BF16),
            (((geo + faces) * width, width), BF16),
            like(basis_tiles),
            like(face_tiles),
            like(state),
            like(right_side),
            like(wall_tile.T),
            like(wall_target),
        ],
        (
            parity,
            next_chip,
            same_chip,
            metric,
            precond,
            neighbors,
            srow,
            basis_tiles,
            face_tiles,
            state,
            right_side,
            wall_tile.T,
            wall_target,
            new_adjoint,
        ),
        (geo + faces + 3) * unit,
        "snnnnnnffffffn",
        copies=6,
    )
    new_state, wall_load = call(
        finish_kernel,
        "finish",
        [((width, elems), BF16), ((nodes, lanes), BF16)],
        [((width, elems), BF16), ((nodes, lanes), BF16)],
        (metric, most, wall_map, elem_hot, node_hot, received),
        2 * unit,
        "nnnnnn",
        out_space=pltpu.HBM,
        copies=elems // (2 * LANES) + 1,
    )
    return (new_state.T, new_adjoint.T, wall_load)


def solution(mesh):
    rows = P(("phase", "elem"), None)
    return jax.shard_map(
        on_device,
        mesh=mesh,
        in_specs=(
            rows,
            rows,
            rows,
            rows,
            P(None, "elem"),
            P("phase", None, None),
            P("phase", None, None),
            P("phase", None),
            P("phase", None),
            P("phase", None),
            rows,
            P("elem", None),
            P("elem"),
            P("elem"),
        ),
        out_specs=(rows, rows, rows),
        check_vma=False,
    )
```

```python
import jax
import jax.numpy as jnp
from jax import lax
from jax.experimental import pallas as pl
from jax.experimental.pallas import tpu as pltpu
from jax.sharding import PartitionSpec as P

HALO = 64
LANES = 128
MAIN = 256
CAP = 8
NOWHERE = -1000.0
F32 = jnp.float32
BF16 = jnp.bfloat16
NT = (((1,), (1,)), ((), ()))
TN = (((0,), (0,)), ((), ()))


def mm(left, right):
    return jnp.dot(left, right, preferred_element_type=F32)


def mm_nt(left, right):
    return lax.dot_general(left, right, NT, preferred_element_type=F32)


def mm_tn(left, right):
    return lax.dot_general(left, right, TN, preferred_element_type=F32)


def lane(rows, width=LANES):
    return lax.broadcasted_iota(jnp.int32, (rows, width), 1)


def hot(left, right):
    return jnp.where(left == right, 1.0, 0.0).astype(BF16)


def half_roll(x):
    return jnp.concatenate([x[:, HALO:], x[:, :HALO]], axis=1)


def columns_of(rows):
    fill = jnp.zeros((LANES - rows.shape[0], rows.shape[1]), F32)
    return jnp.transpose(jnp.concatenate([rows, fill], axis=0))


def transposed(x):
    m, n = x.shape
    x = x.astype(F32)
    if m % LANES:
        x = jnp.concatenate([x, jnp.zeros((LANES - m % LANES, n), F32)], axis=0)
    if n % LANES:
        x = jnp.concatenate([x, jnp.zeros((x.shape[0], LANES - n % LANES), F32)], axis=1)
    return jnp.transpose(x)[:n, :m]


def offsets(neighbors, first, elems):
    position = first + lax.broadcasted_iota(jnp.int32, neighbors.shape, 1)
    distance = ((neighbors - position + HALO) & (elems - 1)) - HALO
    return distance, neighbors >= 0, position


def padded_rows(x, rows):
    return jnp.concatenate([x, jnp.zeros((rows - x.shape[0], x.shape[1]), x.dtype)], axis=0)


def key_column(key_row):
    return jnp.transpose(jnp.broadcast_to(key_row, (LANES, key_row.shape[1])))[:, :1]


def rank_row(key_row, base_row):
    column = key_column(key_row)
    return jnp.sum(jnp.where((column < key_row) & (column >= base_row), 1.0, 0.0), axis=0, keepdims=True)


def rank_column(key_row, base_row):
    key, base = key_column(key_row), key_column(base_row)
    return jnp.sum(jnp.where((key_row < key) & (key_row >= base), 1.0, 0.0), axis=1, keepdims=True)


def node_keys(target, elems):
    nodes = target.shape[1]
    device = (target // elems).astype(F32)
    key = device * nodes + lax.broadcasted_iota(jnp.int32, (1, nodes), 1).astype(F32)
    return device, key, device * nodes


def adjoint_halo(parity, same_chip, next_chip):
    mask = (lane(same_chip.shape[0]) < HALO).astype(jnp.int32) != parity
    return jnp.where(mask, next_chip.astype(F32), same_chip.astype(F32))


def state_halo(parity, same_chip, next_chip):
    mask = (lane(same_chip.shape[0]) < HALO).astype(jnp.int32) != parity
    return jnp.where(mask, same_chip.astype(F32), next_chip.astype(F32))


def begin(copies, sems):
    started = [pltpu.make_async_copy(a, b, sems.at[i]) for i, (a, b) in enumerate(copies)]
    for copy in started:
        copy.start()
    return started


def load_kernel(
    state_hbm, adjoint_hbm, neighbors_hbm, state_ends_ref, adjoint_ends_ref, neighbors_ref, sems
):
    last = state_hbm.shape[1] - LANES
    pairs = [(neighbors_hbm, neighbors_ref)]
    for far, near in ((state_hbm, state_ends_ref), (adjoint_hbm, adjoint_ends_ref)):
        pairs.append((far.at[:, :LANES], near.at[:, :LANES]))
        pairs.append((far.at[:, last:], near.at[:, LANES:]))
    for copy in begin(pairs, sems):
        copy.wait()


def pack_kernel(
    parity_ref, state_ends_ref, adjoint_ends_ref, neighbors_ref, same_chip_ref, next_chip_ref
):
    width, elems = adjoint_ends_ref.shape[0], neighbors_ref.shape[1]
    final = elems - LANES
    low = lane(width) < HALO
    rows = same_chip_ref.shape[0] - width

    def codes(first):
        distance, linked, _ = offsets(neighbors_ref[:, first : first + LANES], first, elems)
        code = jnp.where(linked, distance + (HALO + 1), 0).astype(F32)
        return half_roll(padded_rows(code, rows)).astype(BF16)

    def adjoint(first):
        return half_roll(adjoint_ends_ref[:, first : first + LANES].astype(F32))

    up_code, down_code = codes(final), codes(0)
    up = jnp.where(low, adjoint(LANES), state_ends_ref[:, LANES:].astype(F32)).astype(BF16)
    down = jnp.where(low, state_ends_ref[:, :LANES].astype(F32), adjoint(0)).astype(BF16)

    @pl.when(parity_ref[0] == 0)
    def _():
        same_chip_ref[:width, :], same_chip_ref[width:, :] = up, up_code
        next_chip_ref[:width, :], next_chip_ref[width:, :] = down, down_code

    @pl.when(parity_ref[0] != 0)
    def _():
        same_chip_ref[:width, :], same_chip_ref[width:, :] = down, down_code
        next_chip_ref[:width, :], next_chip_ref[width:, :] = up, up_code


def spread(x_ref, first, count, lanes, gathered):
    for f in range(count):
        one = gathered[:, f * LANES : (f + 1) * LANES].astype(BF16)
        rest = one.shape[0] - MAIN
        x_ref[first + f * MAIN : first + (f + 1) * MAIN, lanes] = one[:MAIN, :]
        start = first + count * MAIN + f * rest
        x_ref[start : start + rest, lanes] = one[MAIN:, :]


def side_by_side(w_ref, tiles_ref):
    count, width, _ = tiles_ref.shape
    for k in range(count):
        w_ref[:, k * MAIN : (k + 1) * MAIN] = tiles_ref[k, :, :MAIN]
    w_ref[:, count * MAIN :] = jnp.concatenate(
        [tiles_ref[k, :, MAIN:] for k in range(count)], axis=1
    )


def inner_kernel(
    adjoint_ref,
    neighbors_ref,
    source_ref,
    metric_ref,
    basis_ref,
    faces_ref,
    precond_ref,
    traction_tile_ref,
    mode_ref,
    wall_node_ref,
    wall_target_ref,
    partial_ref,
    inner_ref,
    w_faces_ref,
    traction_map_ref,
    edge_traction_ref,
    edge_inverse_ref,
    edge_hot_ref,
    srow_ref,
    out_modes_ref,
    out_traction_ref,
    metric_out_ref,
    precond_out_ref,
    x_ref,
    w_ref,
):
    width, elems = adjoint_ref.shape
    geo, count = basis_ref.shape[0], faces_ref.shape[0]
    tail = width - MAIN
    nodes, lanes = mode_ref.shape
    distance, linked, position = offsets(neighbors_ref[...], 0, elems)
    target = jnp.where(linked, (position + distance).astype(F32), NOWHERE)
    span = LANES + 2 * HALO
    base = geo * width
    for b in range(elems // LANES):
        start = min(max(b * LANES - HALO, 0), elems - span)
        row = b * LANES + lax.broadcasted_iota(jnp.int32, (LANES, span), 0)
        named = jnp.concatenate(
            [hot(row.astype(F32), target[f : f + 1, start : start + span]) for f in range(count)],
            axis=0,
        )
        gathered = mm_nt(adjoint_ref[:, start : start + span], named)
        spread(x_ref, base, count, slice(b * LANES, (b + 1) * LANES), gathered)

    value = adjoint_ref[...].astype(F32)
    for k in range(geo):
        scaled = (value * metric_ref[k : k + 1, :]).astype(BF16)
        x_ref[k * MAIN : (k + 1) * MAIN, :] = scaled[:MAIN, :]
        start = geo * MAIN + k * tail
        x_ref[start : start + tail, :] = scaled[MAIN:, :]
    side_by_side(w_faces_ref, faces_ref)
    total = mm(w_faces_ref[...], x_ref[base:, :])
    side_by_side(w_ref, basis_ref)
    total += mm(w_ref[...], x_ref[:base, :])
    metric_out_ref[...] = metric_ref[...]
    precond_out_ref[...] = precond_ref[...]

    node = wall_node_ref[...]
    on_wall = node >= 0
    owner = jnp.where(on_wall, node // nodes, 0).astype(F32)
    elem_slot = owner * CAP + rank_row(node.astype(F32), owner * nodes)
    elem_slot = jnp.where(on_wall, elem_slot, NOWHERE)
    device, key, key_base = node_keys(wall_target_ref[...], elems)
    node_slot = device * CAP + rank_row(key, key_base)
    srow_ref[...] = jnp.zeros(srow_ref.shape, F32)
    srow_ref[0:1, :] = elem_slot
    srow_ref[1:2, :nodes] = node_slot
    slots = out_modes_ref.shape[0]
    place = lax.broadcasted_iota(jnp.int32, (slots, nodes), 0).astype(F32)
    out_modes_ref[...] = mm(hot(place, node_slot), mode_ref[...])

    rest = source_ref[...].astype(F32) - total
    last = elems - LANES
    partial_ref[:, :LANES] = rest[:, :LANES]
    partial_ref[:, LANES:] = rest[:, last:]

    traction_t = transposed(traction_tile_ref[...]).astype(BF16)
    update = mm(precond_ref[...], rest[:, LANES:last].astype(BF16))
    inverse = 1.0 / metric_ref[0:1, :]
    edge_inverse = jnp.concatenate([inverse[:, :LANES], inverse[:, last:]], axis=1)
    edge_inverse_ref[...] = edge_inverse

    both = mm(traction_t, precond_ref[...])
    coarse = both.astype(BF16)
    two_parts = jnp.concatenate([coarse, (both - coarse.astype(F32)).astype(BF16)], axis=0)
    product = mm(two_parts, w_faces_ref[...])
    traction_map_ref[...] = (product[:lanes, :] + product[lanes:, :]).astype(BF16)
    for k, first in enumerate((0, last)):
        at = slice(k * LANES, (k + 1) * LANES)
        own = mm(two_parts, rest[:, first : first + LANES].astype(BF16))
        own = (own[:lanes, :] + own[lanes:, :]) * edge_inverse[:, at]
        edge_traction_ref[:, at] = mm(traction_t, adjoint_ref[:, first : first + LANES]) + own
    inner = (value[:, LANES:last] + update * inverse[:, LANES:last]).astype(BF16)
    inner_ref[...] = inner
    traction = mm(traction_t, inner).astype(BF16)

    place = lax.broadcasted_iota(jnp.int32, (slots, last - LANES), 0).astype(F32)
    out_traction_ref[...] = mm_nt(hot(place, elem_slot[:, LANES:last]), traction)
    edge_slot = jnp.concatenate([elem_slot[:, :LANES], elem_slot[:, last:]], axis=1)
    edge_hot_ref[...] = hot(place, edge_slot)


def edge_kernel(
    parity_ref,
    next_chip_ref,
    same_chip_ref,
    traction_map_ref,
    edge_traction_ref,
    edge_inverse_ref,
    edge_hot_ref,
    out_modes_ref,
    out_traction_ref,
    x_ref,
    send_ref,
):
    width = next_chip_ref.shape[0] - 16
    count = x_ref.shape[0] // width
    slots, lanes = out_modes_ref.shape
    message = adjoint_halo(parity_ref[0], same_chip_ref[...], next_chip_ref[...])
    halo, code = message[:width, :].astype(BF16), message[width : width + 8, :]
    position = lane(8)
    shift = jnp.where(position < HALO, -(2 * HALO + 1), -1)
    target = jnp.where(code == 0.0, NOWHERE, code + (position + shift).astype(F32))
    row = lax.broadcasted_iota(jnp.int32, (LANES, LANES), 0).astype(F32)
    named = jnp.concatenate([hot(row, target[f : f + 1, :]) for f in range(count)], axis=0)
    spread(x_ref, 0, count, slice(0, LANES), mm_nt(halo, named))
    owed = mm(traction_map_ref[...], x_ref[...])
    traction = edge_traction_ref[...] - at_the_ends(owed) * edge_inverse_ref[...]
    out_traction = out_traction_ref[...] + mm_nt(edge_hot_ref[...], traction.astype(BF16))
    both = [x.reshape(slots // CAP, CAP, lanes) for x in (out_modes_ref[...], out_traction)]
    send_ref[...] = jnp.concatenate(both, axis=1).reshape(2 * slots, lanes).astype(BF16)


def at_the_ends(owed):
    low = lane(owed.shape[0]) < HALO
    return jnp.concatenate([jnp.where(low, owed, 0.0), jnp.where(low, 0.0, owed)], axis=1)


def adjoint_kernel(
    adjoint_ends_ref,
    partial_ref,
    inner_ref,
    w_faces_ref,
    precond_ref,
    edge_inverse_ref,
    x_ref,
    new_adjoint_ref,
):
    last = new_adjoint_ref.shape[1] - LANES
    rest = partial_ref[...] - at_the_ends(mm(w_faces_ref[...], x_ref[...]))
    update = mm(precond_ref[...], rest.astype(BF16)) * edge_inverse_ref[...]
    edge = (adjoint_ends_ref[...].astype(F32) + update).astype(BF16)
    new_adjoint_ref[:, :LANES] = edge[:, :LANES]
    new_adjoint_ref[:, LANES:last] = inner_ref[...]
    new_adjoint_ref[:, last:] = edge[:, LANES:]


def forward_kernel(
    parity_ref,
    next_chip_ref,
    same_chip_ref,
    metric_ref,
    precond_ref,
    neighbors_ref,
    srow_ref,
    basis_hbm,
    faces_hbm,
    state_hbm,
    right_hbm,
    wall_tile_t_hbm,
    wall_target_hbm,
    after_hbm,
    most_ref,
    wall_map_ref,
    elem_hot_ref,
    node_hot_ref,
    x_ref,
    w_ref,
    basis_ref,
    faces_ref,
    state_ref,
    right_ref,
    wall_tile_t_ref,
    wall_target_ref,
    sems,
):
    width, elems = state_ref.shape
    copies = begin(
        [
            (state_hbm, state_ref),
            (right_hbm, right_ref),
            (wall_tile_t_hbm, wall_tile_t_ref),
            (wall_target_hbm, wall_target_ref),
            (faces_hbm, faces_ref),
            (basis_hbm, basis_ref),
        ],
        sems,
    )
    copies[0].wait()
    geo, count = basis_ref.shape[0], faces_ref.shape[0]
    tail = width - MAIN
    base = geo * width
    factors = columns_of(metric_ref[...])
    value = transposed(state_ref[...])
    tails = []
    for k in range(geo):
        scaled = (value * factors[:, k : k + 1]).astype(BF16)
        x_ref[:, k * MAIN : (k + 1) * MAIN] = scaled[:, :MAIN]
        tails.append(scaled[:, MAIN:])
    x_ref[:, geo * MAIN : base] = jnp.concatenate(tails, axis=1)

    distance, linked, position = offsets(neighbors_ref[...], 0, elems)
    source = position + distance
    span = LANES + 2 * HALO
    last = elems - LANES
    block = position // LANES
    shift = jnp.where(
        position < LANES,
        jnp.where(source < 0, span, 0),
        jnp.where(
            position >= last,
            jnp.where(source >= elems, -elems, span - elems),
            HALO - block * LANES,
        ),
    )
    column = columns_of(padded_rows(jnp.where(linked, (source + shift).astype(F32), NOWHERE), 8))
    halo = state_halo(parity_ref[0], same_chip_ref[...], next_chip_ref[...])[:width, :].astype(BF16)
    place = lane(LANES, span).astype(F32)
    for b in range(elems // LANES):
        if b == 0:
            beside = jnp.concatenate([state_ref[:, : span - HALO], halo[:, HALO:]], axis=1)
        elif b == elems // LANES - 1:
            beside = jnp.concatenate([halo[:, :HALO], state_ref[:, elems - span + HALO :]], axis=1)
        else:
            beside = state_ref[:, b * LANES - HALO : b * LANES - HALO + span]
        rows = slice(b * LANES, (b + 1) * LANES)
        named = jnp.concatenate([hot(place, column[rows, f : f + 1]) for f in range(count)], axis=0)
        gathered = mm_nt(named, beside).astype(BF16)
        tails = []
        for f in range(count):
            one = gathered[f * LANES : (f + 1) * LANES, :]
            x_ref[rows, base + f * MAIN : base + (f + 1) * MAIN] = one[:, :MAIN]
            tails.append(one[:, MAIN:])
        x_ref[rows, base + count * MAIN :] = jnp.concatenate(tails, axis=1)

    for copy in copies[1:]:
        copy.wait()
    for first, tiles_ref in ((0, basis_ref), (base, faces_ref)):
        number = tiles_ref.shape[0]
        for k in range(number):
            w_ref[first + k * MAIN : first + (k + 1) * MAIN, :] = tiles_ref[k, :MAIN, :]
            start = first + number * MAIN + k * tail
            w_ref[start : start + tail, :] = tiles_ref[k, MAIN:, :]
    applied = mm(x_ref[...], w_ref[...])
    rest = (right_ref[...].astype(F32) - transposed(applied)).astype(BF16)

    precond_t = transposed(precond_ref[...]).astype(BF16)
    inverse = 1.0 / metric_ref[0:1, :]
    most_ref[...] = state_ref[...].astype(F32) + mm(precond_t, rest) * inverse
    wall_map_ref[...] = mm(precond_t, wall_tile_t_ref[...]).astype(BF16)
    slots = elem_hot_ref.shape[0]
    nodes = node_hot_ref.shape[0]
    place = lax.broadcasted_iota(jnp.int32, (slots, elems), 0).astype(F32)
    elem_hot_ref[...] = hot(place, srow_ref[0:1, :])
    device, key, key_base = node_keys(wall_target_ref[...], elems)
    node_slot = key_column(device) * CAP + rank_column(key, key_base)
    node_hot_ref[...] = hot(lane(nodes, slots).astype(F32), node_slot)


def finish_kernel(
    metric_ref,
    most_ref,
    wall_map_ref,
    elem_hot_ref,
    node_hot_ref,
    received_ref,
    new_state_hbm,
    wall_load_hbm,
    new_state_ref,
    wall_load_ref,
    sems,
):
    slots, lanes = elem_hot_ref.shape[0], received_ref.shape[1]
    elems = most_ref.shape[1]
    received = received_ref[...].astype(F32).reshape(slots // CAP, 2 * CAP, lanes)
    modes = received[:, :CAP, :].reshape(slots, lanes).astype(BF16)
    traction = received[:, CAP:, :].reshape(slots, lanes).astype(BF16)
    inverse = 1.0 / metric_ref[0:1, :]
    copies = []
    step = 2 * LANES
    for first in range(0, elems, step):
        part = slice(first, first + step)
        wall_modes_t = mm_tn(modes, elem_hot_ref[:, part]).astype(BF16)
        update = mm(wall_map_ref[...], wall_modes_t)
        new_state_ref[:, part] = (most_ref[:, part] + update * inverse[:, part]).astype(BF16)
        pair = (new_state_ref.at[:, part], new_state_hbm.at[:, part])
        copies += begin([pair], sems.at[first // step : first // step + 1])
    wall_load_ref[...] = mm(node_hot_ref[...], traction).astype(BF16)
    count = len(copies)
    copies += begin([(wall_load_ref, wall_load_hbm)], sems.at[count : count + 1])
    for copy in copies:
        copy.wait()


NEAR = pl.BlockSpec(memory_space=pltpu.VMEM)
FAR = pl.BlockSpec(memory_space=pltpu.HBM)
SCALAR = pl.BlockSpec(memory_space=pltpu.SMEM)


def call(kernel, name, outs, scratch, args, flops, specs, out_space=pltpu.VMEM, copies=0):
    size = sum(a.size * a.dtype.itemsize for a in args)
    sems = [pltpu.SemaphoreType.DMA((copies,))] if copies else []
    spec_of = {"s": SCALAR, "n": NEAR, "f": FAR}
    space_of = {"n": pltpu.VMEM, "f": pltpu.HBM}
    args = [
        pltpu.with_memory_space_constraint(a, space_of[c]) if c in space_of else a
        for a, c in zip(args, specs, strict=True)
    ]
    return pl.pallas_call(
        kernel,
        out_shape=[out_space(shape, dtype) for shape, dtype in outs],
        in_specs=[spec_of[c] for c in specs],
        out_specs=[pl.BlockSpec(memory_space=out_space)] * len(outs),
        scratch_shapes=[pltpu.VMEM(shape, dtype) for shape, dtype in scratch] + sems,
        compiler_params=pltpu.CompilerParams(vmem_limit_bytes=28 * 1024 * 1024),
        cost_estimate=pl.CostEstimate(flops=flops, bytes_accessed=size, transcendentals=0),
        name=name,
    )(*args)


def on_device(
    state,
    adjoint,
    right_side,
    source,
    metric,
    basis_tiles,
    face_tiles,
    precond,
    wall_tile,
    traction_tile,
    mode_rows,
    neighbors,
    wall_node,
    wall_target,
):
    elems, width = state.shape
    nodes, lanes = mode_rows.shape
    geo, faces = basis_tiles.shape[0], face_tiles.shape[0]
    devices = lax.axis_size("elem")
    slots = devices * CAP
    state, adjoint, right_side, source = state.T, adjoint.T, right_side.T, source.T
    neighbors = neighbors.T
    wall_node, wall_target = wall_node.reshape(1, elems), wall_target.reshape(1, nodes)
    parity = (lax.axis_index("elem") % 2).reshape(1)
    unit = 2 * elems * width * width

    def like(x):
        return (x.shape, x.dtype)

    message = ((width + 16, LANES), BF16)
    ends = ((width, 2 * LANES), BF16)
    state_ends, adjoint_ends, neighbors = call(
        load_kernel,
        "load",
        [ends, ends, like(neighbors)],
        [],
        (state, adjoint, neighbors),
        1000,
        "fff",
        copies=5,
    )
    same_chip, next_chip = call(
        pack_kernel,
        "pack",
        [message, message],
        [],
        (parity, state_ends, adjoint_ends, neighbors),
        10**10,
        "snnn",
    )
    pairs = [(i, i + 1) for i in range(1, devices - 1, 2)]
    next_chip = lax.ppermute(next_chip, "elem", pairs + [(j, i) for i, j in pairs])
    pairs = [(i, i + 1) for i in range(0, devices, 2)]
    same_chip = lax.ppermute(same_chip, "elem", pairs + [(j, i) for i, j in pairs])

    (
        partial,
        inner,
        w_faces,
        traction_map,
        edge_traction,
        edge_inverse,
        edge_hot,
        srow,
        out_modes,
        out_traction,
        metric,
        precond,
    ) = call(
        inner_kernel,
        "inner",
        [
            ((width, 2 * LANES), F32),
            ((width, elems - 2 * LANES), BF16),
            ((width, faces * width), BF16),
            ((lanes, faces * width), BF16),
            ((lanes, 2 * LANES), F32),
            ((1, 2 * LANES), F32),
            ((slots, 2 * LANES), BF16),
            ((8, elems), F32),
            ((slots, lanes), F32),
            ((slots, lanes), F32),
            like(metric),
            like(precond),
        ],
        [
            (((geo + faces) * width, elems), BF16),
            ((width, geo * width), BF16),
        ],
        (
            adjoint,
            neighbors,
            source,
            metric,
            basis_tiles,
            face_tiles,
            precond,
            traction_tile,
            mode_rows,
            wall_node,
            wall_target,
        ),
        (geo + faces + 3) * unit,
        "nnnnnnnnnnn",
    )
    x, send = call(
        edge_kernel,
        "edge",
        [((faces * width, LANES), BF16), ((2 * slots, lanes), BF16)],
        [],
        (
            parity,
            next_chip,
            same_chip,
            traction_map,
            edge_traction,
            edge_inverse,
            edge_hot,
            out_modes,
            out_traction,
        ),
        unit,
        "snnnnnnnn",
    )
    received = lax.all_to_all(send, "elem", 0, 0, tiled=True)
    (new_adjoint,) = call(
        adjoint_kernel,
        "adjoint",
        [((width, elems), BF16)],
        [],
        (adjoint_ends, partial, inner, w_faces, precond, edge_inverse, x),
        2 * unit,
        "nnnnnnn",
    )
    most, wall_map, elem_hot, node_hot = call(
        forward_kernel,
        "forward",
        [
            ((width, elems), F32),
            ((width, lanes), BF16),
            ((slots, elems), BF16),
            ((nodes, slots), BF16),
        ],
        [
            ((elems, (geo + faces) * width), BF16),
            (((geo + faces) * width, width), BF16),
            like(basis_tiles),
            like(face_tiles),
            like(state),
            like(right_side),
            like(wall_tile.T),
            like(wall_target),
        ],
        (
            parity,
            next_chip,
            same_chip,
            metric,
            precond,
            neighbors,
            srow,
            basis_tiles,
            face_tiles,
            state,
            right_side,
            wall_tile.T,
            wall_target,
            x,
        ),
        (geo + faces + 3) * unit,
        "snnnnnnffffffn",
        copies=6,
    )
    new_state, wall_load = call(
        finish_kernel,
        "finish",
        [((width, elems), BF16), ((nodes, lanes), BF16)],
        [((width, elems), BF16), ((nodes, lanes), BF16)],
        (metric, most, wall_map, elem_hot, node_hot, received),
        2 * unit,
        "nnnnnn",
        out_space=pltpu.HBM,
        copies=elems // (2 * LANES) + 1,
    )
    return (new_state.T, new_adjoint.T, wall_load)


def solution(mesh):
    rows = P(("phase", "elem"), None)
    return jax.shard_map(
        on_device,
        mesh=mesh,
        in_specs=(
            rows,
            rows,
            rows,
            rows,
            P(None, "elem"),
            P("phase", None, None),
            P("phase", None, None),
            P("phase", None),
            P("phase", None),
            P("phase", None),
            rows,
            P("elem", None),
            P("elem"),
            P("elem"),
        ),
        out_specs=(rows, rows, rows),
        check_vma=False,
    )
```

```python
import jax
import jax.numpy as jnp
from jax import lax
from jax.experimental import pallas as pl
from jax.experimental.pallas import tpu as pltpu
from jax.sharding import PartitionSpec as P

HALO = 64
LANES = 128
MAIN = 256
CAP = 8
NOWHERE = -1000.0
F32 = jnp.float32
BF16 = jnp.bfloat16
NT = (((1,), (1,)), ((), ()))
TN = (((0,), (0,)), ((), ()))


def mm(left, right):
    return jnp.dot(left, right, preferred_element_type=F32)


def mm_nt(left, right):
    return lax.dot_general(left, right, NT, preferred_element_type=F32)


def mm_tn(left, right):
    return lax.dot_general(left, right, TN, preferred_element_type=F32)


def lane(rows, width=LANES):
    return lax.broadcasted_iota(jnp.int32, (rows, width), 1)


def hot(left, right):
    return jnp.where(left == right, 1.0, 0.0).astype(BF16)


def half_roll(x):
    return jnp.concatenate([x[:, HALO:], x[:, :HALO]], axis=1)


def columns_of(rows):
    fill = jnp.zeros((LANES - rows.shape[0], rows.shape[1]), F32)
    return jnp.transpose(jnp.concatenate([rows, fill], axis=0))


def transposed(x):
    m, n = x.shape
    x = x.astype(F32)
    if m % LANES:
        x = jnp.concatenate([x, jnp.zeros((LANES - m % LANES, n), F32)], axis=0)
    if n % LANES:
        x = jnp.concatenate([x, jnp.zeros((x.shape[0], LANES - n % LANES), F32)], axis=1)
    return jnp.transpose(x)[:n, :m]


def offsets(neighbors, first, elems):
    position = first + lax.broadcasted_iota(jnp.int32, neighbors.shape, 1)
    distance = ((neighbors - position + HALO) & (elems - 1)) - HALO
    return distance, neighbors >= 0, position


def padded_rows(x, rows):
    return jnp.concatenate([x, jnp.zeros((rows - x.shape[0], x.shape[1]), x.dtype)], axis=0)


def key_column(key_row):
    return jnp.transpose(jnp.broadcast_to(key_row, (LANES, key_row.shape[1])))[:, :1]


def rank_row(key_row, base_row):
    column = key_column(key_row)
    return jnp.sum(jnp.where((column < key_row) & (column >= base_row), 1.0, 0.0), axis=0, keepdims=True)


def rank_column(key_row, base_row):
    key, base = key_column(key_row), key_column(base_row)
    return jnp.sum(jnp.where((key_row < key) & (key_row >= base), 1.0, 0.0), axis=1, keepdims=True)


def node_keys(target, elems):
    nodes = target.shape[1]
    device = (target // elems).astype(F32)
    key = device * nodes + lax.broadcasted_iota(jnp.int32, (1, nodes), 1).astype(F32)
    return device, key, device * nodes


def adjoint_halo(parity, same_chip, next_chip):
    mask = (lane(same_chip.shape[0]) < HALO).astype(jnp.int32) != parity
    return jnp.where(mask, next_chip.astype(F32), same_chip.astype(F32))


def state_halo(parity, same_chip, next_chip):
    mask = (lane(same_chip.shape[0]) < HALO).astype(jnp.int32) != parity
    return jnp.where(mask, same_chip.astype(F32), next_chip.astype(F32))


def begin(copies, sems):
    started = [pltpu.make_async_copy(a, b, sems.at[i]) for i, (a, b) in enumerate(copies)]
    for copy in started:
        copy.start()
    return started


def load_kernel(
    state_hbm, adjoint_hbm, neighbors_hbm, state_ends_ref, adjoint_ends_ref, neighbors_ref, sems
):
    last = state_hbm.shape[1] - LANES
    pairs = [(neighbors_hbm, neighbors_ref)]
    for far, near in ((state_hbm, state_ends_ref), (adjoint_hbm, adjoint_ends_ref)):
        pairs.append((far.at[:, :LANES], near.at[:, :LANES]))
        pairs.append((far.at[:, last:], near.at[:, LANES:]))
    for copy in begin(pairs, sems):
        copy.wait()


def pack_kernel(
    parity_ref, state_ends_ref, adjoint_ends_ref, neighbors_ref, same_chip_ref, next_chip_ref
):
    width, elems = adjoint_ends_ref.shape[0], neighbors_ref.shape[1]
    final = elems - LANES
    low = lane(width) < HALO
    rows = same_chip_ref.shape[0] - width

    def codes(first):
        distance, linked, _ = offsets(neighbors_ref[:, first : first + LANES], first, elems)
        code = jnp.where(linked, distance + (HALO + 1), 0).astype(F32)
        return half_roll(padded_rows(code, rows)).astype(BF16)

    def adjoint(first):
        return half_roll(adjoint_ends_ref[:, first : first + LANES].astype(F32))

    up_code, down_code = codes(final), codes(0)
    up = jnp.where(low, adjoint(LANES), state_ends_ref[:, LANES:].astype(F32)).astype(BF16)
    down = jnp.where(low, state_ends_ref[:, :LANES].astype(F32), adjoint(0)).astype(BF16)

    @pl.when(parity_ref[0] == 0)
    def _():
        same_chip_ref[:width, :], same_chip_ref[width:, :] = up, up_code
        next_chip_ref[:width, :], next_chip_ref[width:, :] = down, down_code

    @pl.when(parity_ref[0] != 0)
    def _():
        same_chip_ref[:width, :], same_chip_ref[width:, :] = down, down_code
        next_chip_ref[:width, :], next_chip_ref[width:, :] = up, up_code


def spread(x_ref, first, count, lanes, gathered):
    for f in range(count):
        one = gathered[:, f * LANES : (f + 1) * LANES].astype(BF16)
        rest = one.shape[0] - MAIN
        x_ref[first + f * MAIN : first + (f + 1) * MAIN, lanes] = one[:MAIN, :]
        start = first + count * MAIN + f * rest
        x_ref[start : start + rest, lanes] = one[MAIN:, :]


def side_by_side(w_ref, tiles_ref):
    count, width, _ = tiles_ref.shape
    for k in range(count):
        w_ref[:, k * MAIN : (k + 1) * MAIN] = tiles_ref[k, :, :MAIN]
    w_ref[:, count * MAIN :] = jnp.concatenate(
        [tiles_ref[k, :, MAIN:] for k in range(count)], axis=1
    )


def inner_kernel(
    adjoint_ref,
    neighbors_ref,
    source_ref,
    metric_ref,
    basis_ref,
    faces_ref,
    precond_ref,
    traction_tile_ref,
    mode_ref,
    wall_node_ref,
    wall_target_ref,
    partial_ref,
    inner_ref,
    w_faces_ref,
    traction_map_ref,
    edge_traction_ref,
    edge_inverse_ref,
    edge_hot_ref,
    srow_ref,
    out_modes_ref,
    out_traction_ref,
    metric_out_ref,
    precond_out_ref,
    x_ref,
    w_ref,
):
    width, elems = adjoint_ref.shape
    geo, count = basis_ref.shape[0], faces_ref.shape[0]
    tail = width - MAIN
    nodes, lanes = mode_ref.shape
    distance, linked, position = offsets(neighbors_ref[...], 0, elems)
    target = jnp.where(linked, (position + distance).astype(F32), NOWHERE)
    span = LANES + 2 * HALO
    base = geo * width
    for b in range(elems // LANES):
        start = min(max(b * LANES - HALO, 0), elems - span)
        row = b * LANES + lax.broadcasted_iota(jnp.int32, (LANES, span), 0)
        named = jnp.concatenate(
            [hot(row.astype(F32), target[f : f + 1, start : start + span]) for f in range(count)],
            axis=0,
        )
        gathered = mm_nt(adjoint_ref[:, start : start + span], named)
        spread(x_ref, base, count, slice(b * LANES, (b + 1) * LANES), gathered)

    value = adjoint_ref[...].astype(F32)
    for k in range(geo):
        scaled = (value * metric_ref[k : k + 1, :]).astype(BF16)
        x_ref[k * MAIN : (k + 1) * MAIN, :] = scaled[:MAIN, :]
        start = geo * MAIN + k * tail
        x_ref[start : start + tail, :] = scaled[MAIN:, :]
    side_by_side(w_faces_ref, faces_ref)
    total = mm(w_faces_ref[...], x_ref[base:, :])
    side_by_side(w_ref, basis_ref)
    total += mm(w_ref[...], x_ref[:base, :])
    metric_out_ref[...] = metric_ref[...]
    precond_out_ref[...] = precond_ref[...]

    node = wall_node_ref[...]
    on_wall = node >= 0
    owner = jnp.where(on_wall, node // nodes, 0).astype(F32)
    elem_slot = owner * CAP + rank_row(node.astype(F32), owner * nodes)
    elem_slot = jnp.where(on_wall, elem_slot, NOWHERE)
    device, key, key_base = node_keys(wall_target_ref[...], elems)
    node_slot = device * CAP + rank_row(key, key_base)
    srow_ref[...] = jnp.zeros(srow_ref.shape, F32)
    srow_ref[0:1, :] = elem_slot
    srow_ref[1:2, :nodes] = node_slot
    slots = out_modes_ref.shape[0]
    place = lax.broadcasted_iota(jnp.int32, (slots, nodes), 0).astype(F32)
    out_modes_ref[...] = mm(hot(place, node_slot), mode_ref[...])

    rest = source_ref[...].astype(F32) - total
    last = elems - LANES
    partial_ref[:, :LANES] = rest[:, :LANES]
    partial_ref[:, LANES:] = rest[:, last:]

    traction_t = transposed(traction_tile_ref[...]).astype(BF16)
    update = mm(precond_ref[...], rest[:, LANES:last].astype(BF16))
    inverse = 1.0 / metric_ref[0:1, :]
    edge_inverse = jnp.concatenate([inverse[:, :LANES], inverse[:, last:]], axis=1)
    edge_inverse_ref[...] = edge_inverse

    both = mm(traction_t, precond_ref[...])
    coarse = both.astype(BF16)
    two_parts = jnp.concatenate([coarse, (both - coarse.astype(F32)).astype(BF16)], axis=0)
    traction_map_ref[...] = mm(coarse, w_faces_ref[...]).astype(BF16)
    for k, first in enumerate((0, last)):
        at = slice(k * LANES, (k + 1) * LANES)
        own = mm(two_parts, rest[:, first : first + LANES].astype(BF16))
        own = (own[:lanes, :] + own[lanes:, :]) * edge_inverse[:, at]
        edge_traction_ref[:, at] = mm(traction_t, adjoint_ref[:, first : first + LANES]) + own
    inner = (value[:, LANES:last] + update * inverse[:, LANES:last]).astype(BF16)
    inner_ref[...] = inner
    traction = mm(traction_t, inner).astype(BF16)

    place = lax.broadcasted_iota(jnp.int32, (slots, last - LANES), 0).astype(F32)
    out_traction_ref[...] = mm_nt(hot(place, elem_slot[:, LANES:last]), traction)
    edge_slot = jnp.concatenate([elem_slot[:, :LANES], elem_slot[:, last:]], axis=1)
    edge_hot_ref[...] = hot(place, edge_slot)


def edge_kernel(
    parity_ref,
    next_chip_ref,
    same_chip_ref,
    traction_map_ref,
    edge_traction_ref,
    edge_inverse_ref,
    edge_hot_ref,
    out_modes_ref,
    out_traction_ref,
    x_ref,
    send_ref,
):
    width = next_chip_ref.shape[0] - 16
    count = x_ref.shape[0] // width
    slots, lanes = out_modes_ref.shape
    message = adjoint_halo(parity_ref[0], same_chip_ref[...], next_chip_ref[...])
    halo, code = message[:width, :].astype(BF16), message[width : width + 8, :]
    position = lane(8)
    shift = jnp.where(position < HALO, -(2 * HALO + 1), -1)
    target = jnp.where(code == 0.0, NOWHERE, code + (position + shift).astype(F32))
    row = lax.broadcasted_iota(jnp.int32, (LANES, LANES), 0).astype(F32)
    named = jnp.concatenate([hot(row, target[f : f + 1, :]) for f in range(count)], axis=0)
    spread(x_ref, 0, count, slice(0, LANES), mm_nt(halo, named))
    owed = mm(traction_map_ref[...], x_ref[...])
    traction = edge_traction_ref[...] - at_the_ends(owed) * edge_inverse_ref[...]
    out_traction = out_traction_ref[...] + mm_nt(edge_hot_ref[...], traction.astype(BF16))
    both = [x.reshape(slots // CAP, CAP, lanes) for x in (out_modes_ref[...], out_traction)]
    send_ref[...] = jnp.concatenate(both, axis=1).reshape(2 * slots, lanes).astype(BF16)


def at_the_ends(owed):
    low = lane(owed.shape[0]) < HALO
    return jnp.concatenate([jnp.where(low, owed, 0.0), jnp.where(low, 0.0, owed)], axis=1)


def adjoint_kernel(
    adjoint_ends_ref,
    partial_ref,
    inner_ref,
    w_faces_ref,
    precond_ref,
    edge_inverse_ref,
    x_ref,
    new_adjoint_ref,
):
    last = new_adjoint_ref.shape[1] - LANES
    rest = partial_ref[...] - at_the_ends(mm(w_faces_ref[...], x_ref[...]))
    update = mm(precond_ref[...], rest.astype(BF16)) * edge_inverse_ref[...]
    edge = (adjoint_ends_ref[...].astype(F32) + update).astype(BF16)
    new_adjoint_ref[:, :LANES] = edge[:, :LANES]
    new_adjoint_ref[:, LANES:last] = inner_ref[...]
    new_adjoint_ref[:, last:] = edge[:, LANES:]


def forward_kernel(
    parity_ref,
    next_chip_ref,
    same_chip_ref,
    metric_ref,
    precond_ref,
    neighbors_ref,
    srow_ref,
    basis_hbm,
    faces_hbm,
    state_hbm,
    right_hbm,
    wall_tile_t_hbm,
    wall_target_hbm,
    after_hbm,
    most_ref,
    wall_map_ref,
    elem_hot_ref,
    node_hot_ref,
    x_ref,
    w_ref,
    basis_ref,
    faces_ref,
    state_ref,
    right_ref,
    wall_tile_t_ref,
    wall_target_ref,
    sems,
):
    width, elems = state_ref.shape
    copies = begin(
        [
            (state_hbm, state_ref),
            (right_hbm, right_ref),
            (wall_tile_t_hbm, wall_tile_t_ref),
            (wall_target_hbm, wall_target_ref),
            (faces_hbm, faces_ref),
            (basis_hbm, basis_ref),
        ],
        sems,
    )
    copies[0].wait()
    geo, count = basis_ref.shape[0], faces_ref.shape[0]
    tail = width - MAIN
    base = geo * width
    factors = columns_of(metric_ref[...])
    value = transposed(state_ref[...])
    tails = []
    for k in range(geo):
        scaled = (value * factors[:, k : k + 1]).astype(BF16)
        x_ref[:, k * MAIN : (k + 1) * MAIN] = scaled[:, :MAIN]
        tails.append(scaled[:, MAIN:])
    x_ref[:, geo * MAIN : base] = jnp.concatenate(tails, axis=1)

    distance, linked, position = offsets(neighbors_ref[...], 0, elems)
    source = position + distance
    span = LANES + 2 * HALO
    last = elems - LANES
    block = position // LANES
    shift = jnp.where(
        position < LANES,
        jnp.where(source < 0, span, 0),
        jnp.where(
            position >= last,
            jnp.where(source >= elems, -elems, span - elems),
            HALO - block * LANES,
        ),
    )
    column = columns_of(padded_rows(jnp.where(linked, (source + shift).astype(F32), NOWHERE), 8))
    halo = state_halo(parity_ref[0], same_chip_ref[...], next_chip_ref[...])[:width, :].astype(BF16)
    place = lane(LANES, span).astype(F32)
    for b in range(elems // LANES):
        if b == 0:
            beside = jnp.concatenate([state_ref[:, : span - HALO], halo[:, HALO:]], axis=1)
        elif b == elems // LANES - 1:
            beside = jnp.concatenate([halo[:, :HALO], state_ref[:, elems - span + HALO :]], axis=1)
        else:
            beside = state_ref[:, b * LANES - HALO : b * LANES - HALO + span]
        rows = slice(b * LANES, (b + 1) * LANES)
        named = jnp.concatenate([hot(place, column[rows, f : f + 1]) for f in range(count)], axis=0)
        gathered = mm_nt(named, beside).astype(BF16)
        tails = []
        for f in range(count):
            one = gathered[f * LANES : (f + 1) * LANES, :]
            x_ref[rows, base + f * MAIN : base + (f + 1) * MAIN] = one[:, :MAIN]
            tails.append(one[:, MAIN:])
        x_ref[rows, base + count * MAIN :] = jnp.concatenate(tails, axis=1)

    for copy in copies[1:]:
        copy.wait()
    for first, tiles_ref in ((0, basis_ref), (base, faces_ref)):
        number = tiles_ref.shape[0]
        for k in range(number):
            w_ref[first + k * MAIN : first + (k + 1) * MAIN, :] = tiles_ref[k, :MAIN, :]
            start = first + number * MAIN + k * tail
            w_ref[start : start + tail, :] = tiles_ref[k, MAIN:, :]
    applied = mm(x_ref[...], w_ref[...])
    rest = (right_ref[...].astype(F32) - transposed(applied)).astype(BF16)

    precond_t = transposed(precond_ref[...]).astype(BF16)
    inverse = 1.0 / metric_ref[0:1, :]
    most_ref[...] = state_ref[...].astype(F32) + mm(precond_t, rest) * inverse
    wall_map_ref[...] = mm(precond_t, wall_tile_t_ref[...]).astype(BF16)
    slots = elem_hot_ref.shape[0]
    nodes = node_hot_ref.shape[0]
    place = lax.broadcasted_iota(jnp.int32, (slots, elems), 0).astype(F32)
    elem_hot_ref[...] = hot(place, srow_ref[0:1, :])
    device, key, key_base = node_keys(wall_target_ref[...], elems)
    node_slot = key_column(device) * CAP + rank_column(key, key_base)
    node_hot_ref[...] = hot(lane(nodes, slots).astype(F32), node_slot)


def finish_kernel(
    metric_ref,
    most_ref,
    wall_map_ref,
    elem_hot_ref,
    node_hot_ref,
    received_ref,
    new_state_hbm,
    wall_load_hbm,
    new_state_ref,
    wall_load_ref,
    sems,
):
    slots, lanes = elem_hot_ref.shape[0], received_ref.shape[1]
    elems = most_ref.shape[1]
    received = received_ref[...].astype(F32).reshape(slots // CAP, 2 * CAP, lanes)
    modes = received[:, :CAP, :].reshape(slots, lanes).astype(BF16)
    traction = received[:, CAP:, :].reshape(slots, lanes).astype(BF16)
    inverse = 1.0 / metric_ref[0:1, :]
    copies = []
    step = 2 * LANES
    for first in range(0, elems, step):
        part = slice(first, first + step)
        wall_modes_t = mm_tn(modes, elem_hot_ref[:, part]).astype(BF16)
        update = mm(wall_map_ref[...], wall_modes_t)
        new_state_ref[:, part] = (most_ref[:, part] + update * inverse[:, part]).astype(BF16)
        pair = (new_state_ref.at[:, part], new_state_hbm.at[:, part])
        copies += begin([pair], sems.at[first // step : first // step + 1])
    wall_load_ref[...] = mm(node_hot_ref[...], traction).astype(BF16)
    count = len(copies)
    copies += begin([(wall_load_ref, wall_load_hbm)], sems.at[count : count + 1])
    for copy in copies:
        copy.wait()


NEAR = pl.BlockSpec(memory_space=pltpu.VMEM)
FAR = pl.BlockSpec(memory_space=pltpu.HBM)
SCALAR = pl.BlockSpec(memory_space=pltpu.SMEM)


def call(kernel, name, outs, scratch, args, flops, specs, out_space=pltpu.VMEM, copies=0):
    size = sum(a.size * a.dtype.itemsize for a in args)
    sems = [pltpu.SemaphoreType.DMA((copies,))] if copies else []
    spec_of = {"s": SCALAR, "n": NEAR, "f": FAR}
    space_of = {"n": pltpu.VMEM, "f": pltpu.HBM}
    args = [
        pltpu.with_memory_space_constraint(a, space_of[c]) if c in space_of else a
        for a, c in zip(args, specs, strict=True)
    ]
    return pl.pallas_call(
        kernel,
        out_shape=[out_space(shape, dtype) for shape, dtype in outs],
        in_specs=[spec_of[c] for c in specs],
        out_specs=[pl.BlockSpec(memory_space=out_space)] * len(outs),
        scratch_shapes=[pltpu.VMEM(shape, dtype) for shape, dtype in scratch] + sems,
        compiler_params=pltpu.CompilerParams(vmem_limit_bytes=28 * 1024 * 1024),
        cost_estimate=pl.CostEstimate(flops=flops, bytes_accessed=size, transcendentals=0),
        name=name,
    )(*args)


def on_device(
    state,
    adjoint,
    right_side,
    source,
    metric,
    basis_tiles,
    face_tiles,
    precond,
    wall_tile,
    traction_tile,
    mode_rows,
    neighbors,
    wall_node,
    wall_target,
):
    elems, width = state.shape
    nodes, lanes = mode_rows.shape
    geo, faces = basis_tiles.shape[0], face_tiles.shape[0]
    devices = lax.axis_size("elem")
    slots = devices * CAP
    state, adjoint, right_side, source = state.T, adjoint.T, right_side.T, source.T
    neighbors = neighbors.T
    wall_node, wall_target = wall_node.reshape(1, elems), wall_target.reshape(1, nodes)
    parity = (lax.axis_index("elem") % 2).reshape(1)
    unit = 2 * elems * width * width

    def like(x):
        return (x.shape, x.dtype)

    message = ((width + 16, LANES), BF16)
    ends = ((width, 2 * LANES), BF16)
    state_ends, adjoint_ends, neighbors = call(
        load_kernel,
        "load",
        [ends, ends, like(neighbors)],
        [],
        (state, adjoint, neighbors),
        1000,
        "fff",
        copies=5,
    )
    same_chip, next_chip = call(
        pack_kernel,
        "pack",
        [message, message],
        [],
        (parity, state_ends, adjoint_ends, neighbors),
        10**10,
        "snnn",
    )
    pairs = [(i, i + 1) for i in range(1, devices - 1, 2)]
    next_chip = lax.ppermute(next_chip, "elem", pairs + [(j, i) for i, j in pairs])
    pairs = [(i, i + 1) for i in range(0, devices, 2)]
    same_chip = lax.ppermute(same_chip, "elem", pairs + [(j, i) for i, j in pairs])

    (
        partial,
        inner,
        w_faces,
        traction_map,
        edge_traction,
        edge_inverse,
        edge_hot,
        srow,
        out_modes,
        out_traction,
        metric,
        precond,
    ) = call(
        inner_kernel,
        "inner",
        [
            ((width, 2 * LANES), F32),
            ((width, elems - 2 * LANES), BF16),
            ((width, faces * width), BF16),
            ((lanes, faces * width), BF16),
            ((lanes, 2 * LANES), F32),
            ((1, 2 * LANES), F32),
            ((slots, 2 * LANES), BF16),
            ((8, elems), F32),
            ((slots, lanes), F32),
            ((slots, lanes), F32),
            like(metric),
            like(precond),
        ],
        [
            (((geo + faces) * width, elems), BF16),
            ((width, geo * width), BF16),
        ],
        (
            adjoint,
            neighbors,
            source,
            metric,
            basis_tiles,
            face_tiles,
            precond,
            traction_tile,
            mode_rows,
            wall_node,
            wall_target,
        ),
        (geo + faces + 3) * unit,
        "nnnnnnnnnnn",
    )
    x, send = call(
        edge_kernel,
        "edge",
        [((faces * width, LANES), BF16), ((2 * slots, lanes), BF16)],
        [],
        (
            parity,
            next_chip,
            same_chip,
            traction_map,
            edge_traction,
            edge_inverse,
            edge_hot,
            out_modes,
            out_traction,
        ),
        unit,
        "snnnnnnnn",
    )
    received = lax.all_to_all(send, "elem", 0, 0, tiled=True)
    (new_adjoint,) = call(
        adjoint_kernel,
        "adjoint",
        [((width, elems), BF16)],
        [],
        (adjoint_ends, partial, inner, w_faces, precond, edge_inverse, x),
        2 * unit,
        "nnnnnnn",
    )
    most, wall_map, elem_hot, node_hot = call(
        forward_kernel,
        "forward",
        [
            ((width, elems), F32),
            ((width, lanes), BF16),
            ((slots, elems), BF16),
            ((nodes, slots), BF16),
        ],
        [
            ((elems, (geo + faces) * width), BF16),
            (((geo + faces) * width, width), BF16),
            like(basis_tiles),
            like(face_tiles),
            like(state),
            like(right_side),
            like(wall_tile.T),
            like(wall_target),
        ],
        (
            parity,
            next_chip,
            same_chip,
            metric,
            precond,
            neighbors,
            srow,
            basis_tiles,
            face_tiles,
            state,
            right_side,
            wall_tile.T,
            wall_target,
            x,
        ),
        (geo + faces + 3) * unit,
        "snnnnnnffffffn",
        copies=6,
    )
    new_state, wall_load = call(
        finish_kernel,
        "finish",
        [((width, elems), BF16), ((nodes, lanes), BF16)],
        [((width, elems), BF16), ((nodes, lanes), BF16)],
        (metric, most, wall_map, elem_hot, node_hot, received),
        2 * unit,
        "nnnnnn",
        out_space=pltpu.HBM,
        copies=elems // (2 * LANES) + 1,
    )
    return (new_state.T, new_adjoint.T, wall_load)


def solution(mesh):
    rows = P(("phase", "elem"), None)
    return jax.shard_map(
        on_device,
        mesh=mesh,
        in_specs=(
            rows,
            rows,
            rows,
            rows,
            P(None, "elem"),
            P("phase", None, None),
            P("phase", None, None),
            P("phase", None),
            P("phase", None),
            P("phase", None),
            rows,
            P("elem", None),
            P("elem"),
            P("elem"),
        ),
        out_specs=(rows, rows, rows),
        check_vma=False,
    )
```
